128 devices in a mesh: dp: 16 (over x, y), ctx: 8 (over z, core).
Axes of the slice: x: 4, y: 4, z: 4, core: 2. Of those that a mesh axis runs over, the one named last changes fastest.
Arguments:
- short_queries: bfloat16 [16, 8, 512, 2048], P('dp', 'ctx'), may hold values from -40 to 40
- short_keys: bfloat16 [16, 8, 512, 512], P('dp', 'ctx'), may hold values from -40 to 40
- short_values: bfloat16 [16, 8, 512, 512], P('dp', 'ctx'), may hold values from -6 to 6
- block_fill: int32 [16, 8, 8], P('dp', 'ctx'), may hold values from 32 to 64
- block_home: int32 [16, 8, 8], P('dp', 'ctx'), may hold values from 0 to 15, as said below
- long_queries: bfloat16 [16, 2048, 2048], P('dp', 'ctx'), may hold values from -40 to 40
- long_keys: bfloat16 [16, 2048, 512], P('dp', 'ctx'), may hold values from -40 to 40
- long_values: bfloat16 [16, 2048, 512], P('dp', 'ctx'), may hold values from -6 to 6
- long_docs: int32 [16, 2048], P('dp', 'ctx'), may hold values from 0 to 2, never falling along the last dimension, each value on 1 to 1024 neighbouring positions
Outputs:
- short_out: bfloat16 [16, 8, 512, 2048], P('dp', 'ctx')
- long_out: bfloat16 [16, 2048, 2048], P('dp', 'ctx')
The draws below stay inside these ranges and needn't reach their ends.
Inputs may be any that keep to these rules, and one draw needn't show every extreme that they name: block_home[s, c, b] names a data group; at most 1 block of one device name the same group, and in each column c one group is named by exactly 1 block of every device.
All inputs are finite; a program needn't handle non-finite values.
Results may differ from the reference program's by a relative error of at most 0.004.
Values may be sent and summed in bfloat16 or wider, within the bound.
No kernel may reach another device: no remote copies, remote signals or barrier semaphores. Data moves between devices by JAX's collectives and lax.ppermute only.
A program may use at most 192 MiB of HBM per device.

```python
import math
import jax
import jax.numpy as jnp
import numpy as np
from jax import lax

QH = 16
KVH = 4
HD = 128
BLOCK = 64
SB = 8
CAP = 1
SROWS = 512
LONG = 2048
N_DP = 16
N_CTX = 8


def draw_short_keys(key, part):
    lead_shape = (N_DP, N_CTX, SB * BLOCK)
    key = jax.random.fold_in(key, 11)
    baseline = jax.random.normal(key, lead_shape + (KVH, HD), jnp.float32)
    return jnp.clip(baseline, -40.0, 40.0).reshape(lead_shape + (KVH * HD,)).astype(jnp.bfloat16)


def draw_short_queries(key, part):
    lead_shape = (N_DP, N_CTX, SB * BLOCK)
    key = jax.random.fold_in(key, 13)
    baseline = jax.random.normal(key, lead_shape + (QH, HD), jnp.float32)
    return jnp.clip(baseline, -40.0, 40.0).reshape(lead_shape + (QH * HD,)).astype(jnp.bfloat16)


def draw_long_keys(key, part):
    lead_shape = (N_DP, LONG)
    key = jax.random.fold_in(key, 17)
    baseline = jax.random.normal(key, lead_shape + (KVH, HD), jnp.float32)
    return jnp.clip(baseline, -40.0, 40.0).reshape(lead_shape + (KVH * HD,)).astype(jnp.bfloat16)


def draw_long_queries(key, part):
    lead_shape = (N_DP, LONG)
    key = jax.random.fold_in(key, 19)
    baseline = jax.random.normal(key, lead_shape + (QH, HD), jnp.float32)
    return jnp.clip(baseline, -40.0, 40.0).reshape(lead_shape + (QH * HD,)).astype(jnp.bfloat16)


def draw_block_home(key, part):
    key = jax.random.fold_in(key, 3)
    stream_one, stream_two, stream_three = jax.random.split(key, 3)
    slot_total = N_DP * CAP
    busiest = jax.random.randint(stream_one, (N_CTX,), 0, N_DP)
    slot_index = jnp.arange(slot_total, dtype=jnp.int32)
    slot_group = slot_index // CAP
    scores = jax.random.randint(stream_two, (N_DP, N_CTX, slot_total), 0, 2 ** 20) * slot_total + slot_index
    scores = jnp.where(slot_group[None, None, :] == busiest[None, :, None], slot_index - slot_total, scores)
    chosen = jnp.argsort(scores, axis=-1)[..., :SB].astype(jnp.int32)
    shuffle = jax.random.randint(stream_three, (N_DP, N_CTX, SB), 0, 2 ** 20) * SB + jnp.arange(SB, dtype=jnp.int32)
    placing = jnp.argsort(shuffle, axis=-1)
    picked = jnp.take_along_axis(chosen, placing, axis=-1)
    return (picked // CAP).astype(jnp.int32)


def with_ends(entries, own_key, low, largest):
    place = [jax.random.randint(jax.random.fold_in(own_key, axis), (), 0, length) for axis, length in enumerate(entries.shape)]
    longest = entries.shape.index(max(entries.shape))
    beside = place[:longest] + [(place[longest] + 1) % entries.shape[longest]] + place[longest + 1:]
    return entries.at[tuple(place)].set(low).at[tuple(beside)].set(largest)


def block_levels(own_key, extent, shards, least, top_value):
    def one(dim, shards_of):
        steps = jax.random.uniform(jax.random.fold_in(jax.random.fold_in(own_key, 6), dim), (shards_of,), jnp.float32, least / len(shards), top_value / len(shards))
        return jnp.repeat(jnp.exp(steps), extent[dim] // shards_of).reshape((-1,) + (1,) * (len(extent) - dim - 1))

    loudness = one(*shards[0])
    for cut in shards[1:]:
        loudness = loudness * one(*cut)
    return loudness


def profile(number_of, total, bound, skew):
    portions = [(1 << 20) // math.isqrt(grade ** skew) + 1 for grade in range(2, number_of + 1)]
    surplus, holding = total - bound - (number_of - 1), [1] * (number_of - 1)
    while surplus > 0:
        free = [i for i in range(number_of - 1) if holding[i] < bound]
        mass, budget = sum([portions[i] for i in free]), surplus
        for i in free:
            extra = min(bound - holding[i], max(1, budget * portions[i] // mass), surplus)
            holding[i] = holding[i] + extra
            surplus = surplus - extra
    return np.array([bound] + holding)


def uneven_parts(own_key, amount, total, limit, slope):
    if amount == 2:
        one = jax.random.randint(own_key, (), max(1, total - limit), min(limit, total - 1) + 1)
        return jnp.stack([one, total - one])
    sizes = jnp.asarray(profile(amount, total, limit, slope), jnp.int32)
    twos = (amount - 1) // 2
    source_of, receiver = sizes[1:1 + 2 * twos:2], sizes[2:2 + 2 * twos:2]
    slack = jnp.minimum(source_of - 1, limit - receiver)
    shifted = jax.random.randint(jax.random.fold_in(own_key, 1), (twos,), 0, 1 << 20) % (slack + 1)
    sizes = sizes.at[1:1 + 2 * twos:2].set(source_of - shifted).at[2:2 + 2 * twos:2].set(receiver + shifted)
    return sizes[jax.random.permutation(jax.random.fold_in(own_key, 2), amount)]


def centred(rng, shape, scale, reach, cuts=(), held_as=jnp.bfloat16):
    values = scale * jax.random.normal(rng, shape, jnp.float32)
    if cuts:
        values = values * block_levels(rng, shape, cuts, -0.22, 0.18)
    return jnp.clip(values, -reach, reach).astype(held_as)


def setup_inputs(seed: int = 0) -> dict:
    seeds = jax.random.split(jax.random.key(seed), 10)
    short_queries = draw_short_queries(jax.random.fold_in(seeds[9], 71), 0)
    short_keys = draw_short_keys(jax.random.fold_in(seeds[9], 71), 0)
    short_values = centred(seeds[2], (N_DP, N_CTX, SROWS, KVH * HD), 1.0, 6.0, ((0, 16), (1, 8)))
    block_fill = with_ends(jax.random.randint(seeds[3], (N_DP, N_CTX, SB), BLOCK // 2, BLOCK + 1), jax.random.fold_in(seeds[3], 1), BLOCK // 2, BLOCK).astype(jnp.int32)
    block_home = draw_block_home(jax.random.fold_in(seeds[9], 71), 0)
    long_queries = draw_long_queries(jax.random.fold_in(seeds[9], 71), 0)
    long_keys = draw_long_keys(jax.random.fold_in(seeds[9], 71), 0)
    long_values = centred(seeds[7], (N_DP, LONG, KVH * HD), 1.0, 6.0, ((0, 16), (1, 8)))
    long_docs = jax.vmap(lambda own: jnp.searchsorted(jnp.cumsum(uneven_parts(own, 3, LONG, LONG // 2, 2)), jnp.arange(LONG), side="right"))(jax.random.split(seeds[8], N_DP)).reshape((N_DP, LONG)).astype(jnp.int32)
    return dict(short_queries=short_queries, short_keys=short_keys, short_values=short_values, block_fill=block_fill, block_home=block_home, long_queries=long_queries, long_keys=long_keys, long_values=long_values, long_docs=long_docs)


masked_score = -1e30


def attend_exact(queries, key_rows, value_rows, allowed):
    count_rows = queries.shape[0]
    grouped = queries.reshape(count_rows, KVH, QH // KVH, HD).astype(jnp.float32)
    key_heads = key_rows.reshape(-1, KVH, HD).astype(jnp.float32)
    value_heads = value_rows.reshape(-1, KVH, HD).astype(jnp.float32)
    scores = jnp.einsum("qhgd,khd->hgqk", grouped, key_heads, precision=lax.Precision.HIGHEST) * (HD ** -0.5)
    scores = jnp.where(allowed[None, None], scores, masked_score)
    row_max = jnp.max(scores, axis=-1, keepdims=True)
    weights = jnp.exp(scores - row_max)
    totals = jnp.sum(weights, axis=-1)
    rounded = lax.optimization_barrier(weights.astype(jnp.bfloat16)).astype(jnp.float32)
    mixture = jnp.einsum("hgqk,khd->qhgd", rounded, value_heads, precision=lax.Precision.HIGHEST)
    mixture = mixture / jnp.transpose(totals, (2, 0, 1))[..., None]
    return mixture.reshape(count_rows, QH * HD)


def short_column(column):
    queries, key_rows, value_rows, fill_counts, homes = column
    blocks = N_DP * SB
    row_count = blocks * BLOCK
    sort_order = jnp.argsort(homes.reshape(blocks) * blocks + jnp.arange(blocks, dtype=jnp.int32))

    def arrange(data, last_width):
        return data.reshape(blocks, BLOCK, last_width)[sort_order].reshape(row_count, last_width)

    query_sorted = arrange(queries, QH * HD)
    key_sorted = arrange(key_rows, KVH * HD)
    value_sorted = arrange(value_rows, KVH * HD)
    doc_rows = jnp.repeat(homes.reshape(blocks)[sort_order], BLOCK)
    usable = (jnp.arange(BLOCK, dtype=jnp.int32)[None, :] < fill_counts.reshape(blocks)[sort_order][:, None]).reshape(row_count)
    block_width = min(512, row_count)
    window = min(row_count, N_DP * CAP * BLOCK + block_width)

    def one_block(block_index):
        first_row = block_index * block_width
        key_first = jnp.clip(first_row + block_width - window, 0, row_count - window)
        query_pos = first_row + jnp.arange(block_width, dtype=jnp.int32)
        key_pos = key_first + jnp.arange(window, dtype=jnp.int32)
        query_docs = lax.dynamic_slice_in_dim(doc_rows, first_row, block_width, 0)
        key_docs = lax.dynamic_slice_in_dim(doc_rows, key_first, window, 0)
        key_usable = lax.dynamic_slice_in_dim(usable, key_first, window, 0)
        query_usable = lax.dynamic_slice_in_dim(usable, first_row, block_width, 0)
        allowed = (key_pos[None, :] <= query_pos[:, None]) & (key_docs[None, :] == query_docs[:, None]) & key_usable[None, :]
        result = attend_exact(
            lax.dynamic_slice_in_dim(query_sorted, first_row, block_width, 0),
            lax.dynamic_slice_in_dim(key_sorted, key_first, window, 0),
            lax.dynamic_slice_in_dim(value_sorted, key_first, window, 0),
            allowed)
        return jnp.where(query_usable[:, None], result, 0.0)

    results = lax.map(one_block, jnp.arange(row_count // block_width, dtype=jnp.int32))
    results = results.reshape(blocks, BLOCK, QH * HD)
    inverse = jnp.argsort(sort_order)
    return results[inverse].reshape(N_DP, SB * BLOCK, QH * HD).astype(jnp.bfloat16)


def long_group(group_data):
    queries, key_rows, value_rows, doc_ids = group_data
    row_count = queries.shape[0]
    block_width = min(512, row_count)
    pieces = []
    for first_row in range(0, row_count, block_width):
        last_row = first_row + block_width
        key_pos = jnp.arange(last_row, dtype=jnp.int32)
        query_pos = first_row + jnp.arange(block_width, dtype=jnp.int32)
        allowed = (key_pos[None, :] <= query_pos[:, None]) & (doc_ids[None, :last_row] == doc_ids[first_row:last_row, None])
        pieces.append(attend_exact(queries[first_row:last_row], key_rows[:last_row], value_rows[:last_row], allowed))
    return jnp.concatenate(pieces, axis=0).astype(jnp.bfloat16)


def reference(short_queries, short_keys, short_values, block_fill, block_home, long_queries, long_keys, long_values, long_docs):
    columns = (jnp.moveaxis(short_queries, 1, 0), jnp.moveaxis(short_keys, 1, 0), jnp.moveaxis(short_values, 1, 0),
               jnp.moveaxis(block_fill, 1, 0), jnp.moveaxis(block_home, 1, 0))
    short_out = jnp.moveaxis(lax.map(short_column, columns), 0, 1)
    long_out = lax.map(long_group, (long_queries, long_keys, long_values, long_docs))
    return short_out, long_out
```

```python
import functools

import jax
import jax.numpy as jnp
from jax import lax
from jax.experimental import pallas as pl
from jax.experimental.pallas import tpu as pltpu
from jax.sharding import PartitionSpec as P

QH = 16
KVH = 4
HD = 128
BLOCK = 64
SB = 8
GROUP = QH // KVH
SIDE = 4
GROUPS = SIDE * SIDE
RANKS = 8
ROWS = SB * BLOCK
LROWS = 256
CHUNK = 4
MASKED = -1e30
SCALE = HD**-0.5 * 1.4426950408889634
MIB = 1024 * 1024

VM = pl.BlockSpec(memory_space=pltpu.VMEM)
SM = pl.BlockSpec(memory_space=pltpu.SMEM)
HB = pl.BlockSpec(memory_space=pl.ANY)


def pairs(step):
    found = []
    for x in range(SIDE):
        for y in range(SIDE):
            for z in range(RANKS // 2):
                for core in range(2):
                    target = step(x, y, z, core)
                    if target is not None:
                        tx, ty, tz, tcore = target
                        found.append(
                            (
                                (x * SIDE + y) * RANKS + z * 2 + core,
                                (tx * SIDE + ty) * RANKS + tz * 2 + tcore,
                            )
                        )
    return found


def send(value, step):
    return lax.ppermute(value, ("dp", "ctx"), pairs(step))


def along_head(k):
    def step(x, y, z, core):
        if core == 0:
            return ((x + k) % SIDE, y, z, core)
        return (x, (y + k) % SIDE, z, core)

    return step


def along_rows(k):
    def step(x, y, z, core):
        if core == 0:
            return (x, (y + k) % SIDE, z, core)
        return ((x + k) % SIDE, y, z, core)

    return step


def up_chips(k):
    def step(x, y, z, core):
        return (x, y, z + k, core) if z + k < RANKS // 2 else None

    return step


def other_core(x, y, z, core):
    return (x, y, z, 1 - core)


def split_kv_kernel(meta, k_ref, v_ref, *outs):
    for k in range(SIDE):
        col = pl.multiple_of(((meta[0] + k) % SIDE) * HD, HD)
        outs[k][:, :HD] = k_ref[:, pl.ds(col, HD)]
        outs[k][:, HD:] = v_ref[:, pl.ds(col, HD)]


def split_kv(meta, keys, values):
    return pl.pallas_call(
        split_kv_kernel,
        out_shape=[jax.ShapeDtypeStruct((ROWS, 2 * HD), jnp.bfloat16)] * SIDE,
        in_specs=[SM, VM, VM],
        out_specs=[VM] * SIDE,
        cost_estimate=pl.CostEstimate(flops=0, bytes_accessed=2 * MIB, transcendentals=0),
    )(meta, keys, values)


def split_q_kernel(meta, q_ref, *outs):
    for k in range(SIDE):
        col = pl.multiple_of(((meta[0] + k) % SIDE) * GROUP * HD, GROUP * HD)
        outs[k][...] = q_ref[:, pl.ds(col, GROUP * HD)]


def split_q(meta, queries):
    width = GROUP * HD
    return pl.pallas_call(
        split_q_kernel,
        grid=(4,),
        out_shape=[jax.ShapeDtypeStruct((ROWS, width), jnp.bfloat16)] * SIDE,
        in_specs=[SM, pl.BlockSpec((ROWS // 4, QH * HD), lambda i: (i, 0))],
        out_specs=[pl.BlockSpec((ROWS // 4, width), lambda i: (i, 0))] * SIDE,
        cost_estimate=pl.CostEstimate(flops=0, bytes_accessed=4 * MIB, transcendentals=0),
    )(meta, queries)


def join_kernel(meta, *refs):
    out_ref = refs[-1]
    for k in range(SIDE):
        col = pl.multiple_of(((meta[0] + k) % SIDE) * GROUP * HD, GROUP * HD)
        out_ref[:, pl.ds(col, GROUP * HD)] = refs[k][...]


def join(meta, pieces):
    width = GROUP * HD
    return pl.pallas_call(
        join_kernel,
        grid=(4,),
        out_shape=jax.ShapeDtypeStruct((ROWS, QH * HD), jnp.bfloat16),
        in_specs=[SM] + [pl.BlockSpec((ROWS // 4, width), lambda i: (i, 0))] * SIDE,
        out_specs=pl.BlockSpec((ROWS // 4, QH * HD), lambda i: (i, 0)),
        cost_estimate=pl.CostEstimate(flops=0, bytes_accessed=4 * MIB, transcendentals=0),
    )(meta, *pieces)


def table_kernel(meta, hf_ref, slot_ref, fill_ref, rank_ref, count_ref):
    head, line, core = meta[0], meta[1], meta[2]

    def clear(i, _):
        slot_ref[i] = 0
        fill_ref[i] = 0
        return 0

    lax.fori_loop(0, GROUPS * GROUPS, clear, 0)
    for d in range(GROUPS):
        count_ref[d] = 0

    def source(s, _):
        high, low = s // SIDE, s % SIDE
        own_head = jnp.where(core == 0, high, low)
        own_line = jnp.where(core == 0, low, high)
        base = (((line - own_line) & 3) * SIDE + ((head - own_head) & 3)) * SB
        for b in range(SB):
            home = hf_ref[s, b]
            rank = count_ref[home]
            count_ref[home] = rank + 1
            rank_ref[s * SB + b] = rank
            slot_ref[home * GROUPS + rank] = base + b
            fill_ref[home * GROUPS + rank] = hf_ref[s, SB + b]
        return 0

    lax.fori_loop(0, GROUPS, source, 0)


def make_tables(meta, hf):
    ints = lambda n: jax.ShapeDtypeStruct((n,), jnp.int32)
    return pl.pallas_call(
        table_kernel,
        out_shape=[ints(GROUPS * GROUPS), ints(GROUPS * GROUPS), ints(GROUPS * SB)],
        in_specs=[SM, SM],
        out_specs=[SM, SM, SM],
        scratch_shapes=[pltpu.SMEM((GROUPS,), jnp.int32)],
        cost_estimate=pl.CostEstimate(flops=4096, bytes_accessed=4096, transcendentals=0),
    )(meta, hf)


def soften(scores, value_rows):
    row_max = jnp.max(scores, axis=-1, keepdims=True)
    weights = jnp.exp2((scores - row_max) * SCALE)
    totals = jnp.sum(weights, axis=-1, keepdims=True)
    mixture = jnp.dot(
        weights.astype(jnp.bfloat16), value_rows, preferred_element_type=jnp.float32
    )
    return mixture / totals


def inner(queries, key_rows):
    return lax.dot_general(
        queries, key_rows, (((1,), (1,)), ((), ())), preferred_element_type=jnp.float32
    )


def short_kernel(shifts, meta, hf_ref, slot_ref, fill_ref, rank_ref, *refs):
    kv_parts = refs[:SIDE]
    q_refs = refs[SIDE : SIDE + len(shifts)]
    out_refs = refs[SIDE + len(shifts) : SIDE + 2 * len(shifts)]
    kv_ref, sems = refs[-2:]
    part_rows = SIDE * ROWS
    copies = [
        pltpu.make_async_copy(
            kv_parts[j], kv_ref.at[pl.ds(j * part_rows, part_rows)], sems.at[j]
        )
        for j in range(SIDE)
    ]
    for copy in copies:
        copy.start()
    for copy in copies:
        copy.wait()
    head, line, core = meta[0], meta[1], meta[2]
    width = CHUNK * BLOCK
    lane = lax.broadcasted_iota(jnp.int32, (1, width), 1)
    lane_block = lane // BLOCK
    lane_row = lane % BLOCK
    row = lax.broadcasted_iota(jnp.int32, (BLOCK, width), 0)

    for position, k in enumerate(shifts):
        q_ref, out_ref = q_refs[position], out_refs[position]
        own_head = (head - k) & 3
        own = jnp.where(core == 0, own_head * SIDE + line, line * SIDE + own_head)

        def one_block(b, _, q_ref=q_ref, out_ref=out_ref, own=own):
            home = hf_ref[own, b]
            own_fill = hf_ref[own, SB + b]
            rank = rank_ref[own * SB + b]
            first = home * GROUPS
            rows = pl.ds(pl.multiple_of(b * BLOCK, BLOCK), BLOCK)

            def attend(chunks):
                q = q_ref[rows, :]
                q = jnp.concatenate(
                    [q[:, h * HD : (h + 1) * HD] for h in range(GROUP)], axis=0
                )
                key_parts, value_parts, biases = [], [], []
                for c in range(chunks):
                    limits = []
                    for j in range(CHUNK):
                        n = c * CHUNK + j
                        start = pl.multiple_of(slot_ref[first + n] * BLOCK, BLOCK)
                        kv = kv_ref[pl.ds(start, BLOCK), :]
                        key_parts.append(kv[:, :HD])
                        value_parts.append(kv[:, HD:])
                        limits.append(jnp.where(n <= rank, fill_ref[first + n], 0))
                    limit = jnp.where(
                        lane_block < 2,
                        jnp.where(lane_block == 0, limits[0], limits[1]),
                        jnp.where(lane_block == 2, limits[2], limits[3]),
                    )
                    if c < chunks - 1:
                        bias = jnp.where(lane_row < limit, 0.0, MASKED)
                        biases.append(jnp.broadcast_to(bias, (BLOCK, width)))
                    else:
                        causal = jnp.where(
                            lane_block == rank - c * CHUNK, row + 1, BLOCK
                        )
                        limit = jnp.minimum(limit, causal)
                        biases.append(jnp.where(lane_row < limit, 0.0, MASKED))
                keys = jnp.concatenate(key_parts, axis=0)
                values = jnp.concatenate(value_parts, axis=0)
                bias = jnp.concatenate(biases, axis=1)
                scores = inner(q, keys) + jnp.concatenate([bias] * GROUP, axis=0)
                mixed = soften(scores, values)
                used = lax.broadcasted_iota(jnp.int32, (BLOCK, HD), 0) < own_fill
                for h in range(GROUP):
                    part = jnp.where(used, mixed[h * BLOCK : (h + 1) * BLOCK], 0.0)
                    out_ref[rows, h * HD : (h + 1) * HD] = part.astype(jnp.bfloat16)

            for chunks in range(1, GROUPS // CHUNK + 1):
                pl.when(rank // CHUNK == chunks - 1)(functools.partial(attend, chunks))
            return 0

        lax.fori_loop(0, SB, one_block, 0)


def short_attention(shifts, meta, hf, tables, kv_parts, q_parts):
    count = len(shifts)
    return pl.pallas_call(
        functools.partial(short_kernel, shifts),
        out_shape=[jax.ShapeDtypeStruct((ROWS, GROUP * HD), jnp.bfloat16)] * count,
        in_specs=[SM] * 5 + [HB] * SIDE + [VM] * count,
        out_specs=[VM] * count,
        scratch_shapes=[
            pltpu.VMEM((GROUPS * ROWS, 2 * HD), jnp.bfloat16),
            pltpu.SemaphoreType.DMA((SIDE,)),
        ],
        compiler_params=pltpu.CompilerParams(vmem_limit_bytes=32 * MIB),
        cost_estimate=pl.CostEstimate(
            flops=count * 700_000_000, bytes_accessed=4 * MIB, transcendentals=count * 1_300_000
        ),
    )(meta, hf, *tables, *kv_parts, *q_parts)


def long_kernel(doc_ref, q_ref, *refs):
    parts = refs[:5]
    out_ref, bias_ref = refs[5:]
    own_doc = doc_ref[...]
    lane = lax.broadcasted_iota(jnp.int32, (LROWS, LROWS), 1)
    row = lax.broadcasted_iota(jnp.int32, (LROWS, LROWS), 0)
    for n in range(5):
        key_doc = parts[n][LROWS : LROWS + 16, :LROWS].astype(jnp.float32)[:1]
        allowed = own_doc == key_doc
        if n == 0:
            allowed = allowed & (lane <= row)
        bias_ref[:, n * LROWS : (n + 1) * LROWS] = jnp.where(allowed, 0.0, MASKED)

    def one_head(h, _):
        col = pl.multiple_of(h * HD, HD)
        vcol = pl.multiple_of((KVH + h) * HD, HD)
        keys = jnp.concatenate([p[:LROWS, pl.ds(col, HD)] for p in parts], axis=0)
        values = jnp.concatenate([p[:LROWS, pl.ds(vcol, HD)] for p in parts], axis=0)
        for i in range(GROUP):
            qcol = pl.multiple_of((h * GROUP + i) * HD, HD)
            scores = inner(q_ref[:, pl.ds(qcol, HD)], keys) + bias_ref[...]
            out_ref[:, pl.ds(qcol, HD)] = soften(scores, values).astype(jnp.bfloat16)
        return 0

    lax.fori_loop(0, KVH, one_head, 0)


def long_attention(docs, queries, parts):
    return pl.pallas_call(
        long_kernel,
        out_shape=jax.ShapeDtypeStruct((LROWS, QH * HD), jnp.bfloat16),
        in_specs=[VM] * 7,
        out_specs=VM,
        scratch_shapes=[pltpu.VMEM((LROWS, 5 * LROWS), jnp.float32)],
        compiler_params=pltpu.CompilerParams(vmem_limit_bytes=32 * MIB),
        cost_estimate=pl.CostEstimate(
            flops=2_700_000_000, bytes_accessed=5 * MIB, transcendentals=5_200_000
        ),
    )(docs, queries, *parts)


def shards(
    short_queries,
    short_keys,
    short_values,
    block_fill,
    block_home,
    long_queries,
    long_keys,
    long_values,
    long_docs,
):
    place, rank = lax.axis_index("dp"), lax.axis_index("ctx")
    core = rank % 2
    head = jnp.where(core == 0, place // SIDE, place % SIDE)
    line = jnp.where(core == 0, place % SIDE, place // SIDE)
    meta = jnp.stack([head, line, core]).astype(jnp.int32)

    kv_own = split_kv(meta, short_keys.reshape(ROWS, KVH * HD), short_values.reshape(ROWS, KVH * HD))
    kv_line = [kv_own[0]] + [send(kv_own[k], along_head(k)) for k in (1, 2, 3)]
    kv_line = jnp.concatenate(kv_line, axis=0)

    q_own = split_q(meta, short_queries.reshape(ROWS, QH * HD))
    q_parts = [q_own[0]] + [send(q_own[k], along_head(k)) for k in (1, 2, 3)]
    kv_parts = [kv_line] + [send(kv_line, along_rows(k)) for k in (1, 2, 3)]

    hf = jnp.concatenate([block_home.reshape(1, SB), block_fill.reshape(1, SB)], axis=1)
    hf = lax.all_gather(hf, "dp", axis=0, tiled=True)
    tables = make_tables(meta, hf)

    docs = long_docs.reshape(1, LROWS).astype(jnp.float32) + 1.0
    doc_rows = jnp.pad(docs.astype(jnp.bfloat16), ((0, 15), (0, 2 * KVH * HD - LROWS)))
    long_own = jnp.concatenate(
        [
            jnp.concatenate(
                [long_keys.reshape(LROWS, KVH * HD), long_values.reshape(LROWS, KVH * HD)], axis=1
            ),
            doc_rows,
        ],
        axis=0,
    )
    long_one = send(long_own, up_chips(1))
    long_two = send(long_own, up_chips(2))
    long_side = send(long_one, other_core)
    long_cross = send(jnp.where(core == 0, long_own, long_two), other_core)
    long_out = long_attention(
        docs.reshape(LROWS, 1),
        long_queries.reshape(LROWS, QH * HD),
        [long_own, long_one, long_two, long_side, long_cross],
    )

    mixed = short_attention((0, 1, 2, 3), meta, hf, tables, kv_parts, q_parts)
    back = [mixed[0]] + [send(mixed[k], along_head(-k)) for k in (1, 2, 3)]
    short_out = join(meta, back)
    return short_out.reshape(short_queries.shape), long_out.reshape(long_queries.shape)


def solution(mesh):
    return jax.shard_map(
        shards,
        mesh=mesh,
        in_specs=(
            P("dp", "ctx", None, None),
            P("dp", "ctx", None, None),
            P("dp", "ctx", None, None),
            P("dp", "ctx", None),
            P("dp", "ctx", None),
            P("dp", "ctx", None),
            P("dp", "ctx", None),
            P("dp", "ctx", None),
            P("dp", "ctx"),
        ),
        out_specs=(P("dp", "ctx", None, None), P("dp", "ctx", None)),
        check_vma=False,
    )
```

```python
import functools

import jax
import jax.numpy as jnp
from jax import lax
from jax.experimental import pallas as pl
from jax.experimental.pallas import tpu as pltpu
from jax.sharding import PartitionSpec as P

QH = 16
KVH = 4
HD = 128
BLOCK = 64
SB = 8
GROUP = QH // KVH
SIDE = 4
GROUPS = SIDE * SIDE
RANKS = 8
ROWS = SB * BLOCK
LROWS = 256
CHUNK = 4
MASKED = -1e30
SCALE = HD**-0.5 * 1.4426950408889634
MIB = 1024 * 1024

VM = pl.BlockSpec(memory_space=pltpu.VMEM)
SM = pl.BlockSpec(memory_space=pltpu.SMEM)
HB = pl.BlockSpec(memory_space=pltpu.HBM)


def pairs(step):
    found = []
    for x in range(SIDE):
        for y in range(SIDE):
            for z in range(RANKS // 2):
                for core in range(2):
                    target = step(x, y, z, core)
                    if target is not None:
                        tx, ty, tz, tcore = target
                        found.append(
                            (
                                (x * SIDE + y) * RANKS + z * 2 + core,
                                (tx * SIDE + ty) * RANKS + tz * 2 + tcore,
                            )
                        )
    return found


def send(value, step):
    return lax.ppermute(value, ("dp", "ctx"), pairs(step))


def along_head(k):
    def step(x, y, z, core):
        if core == 0:
            return ((x + k) % SIDE, y, z, core)
        return (x, (y + k) % SIDE, z, core)

    return step


def along_rows(k):
    def step(x, y, z, core):
        if core == 0:
            return (x, (y + k) % SIDE, z, core)
        return ((x + k) % SIDE, y, z, core)

    return step


def up_chips(k):
    def step(x, y, z, core):
        return (x, y, z + k, core) if z + k < RANKS // 2 else None

    return step


def other_core(x, y, z, core):
    return (x, y, z, 1 - core)


def other_place(bit):
    def step(x, y, z, core):
        place = (x * SIDE + y) ^ bit
        return (place // SIDE, place % SIDE, z, core)

    return step


def split_kernel(width, meta, *refs):
    sources, outs, sems = refs[:-SIDE - 1], refs[-SIDE - 1 : -1], refs[-1]
    copies = []
    for k in range(SIDE):
        col = pl.multiple_of(((meta[0] + k) & 3) * width, width)
        for n, source in enumerate(sources):
            copies.append(
                pltpu.make_async_copy(
                    source.at[:, pl.ds(col, width)],
                    outs[k].at[:, pl.ds(n * width, width)],
                    sems.at[k, n],
                )
            )
    for copy in copies:
        copy.start()
    for copy in copies:
        copy.wait()


def split_heads(meta, *sources):
    width = sources[0].shape[1] // KVH
    total = len(sources) * width
    return pl.pallas_call(
        functools.partial(split_kernel, width),
        out_shape=[jax.ShapeDtypeStruct((ROWS, total), jnp.bfloat16)] * SIDE,
        in_specs=[SM] + [HB] * len(sources),
        out_specs=[HB] * SIDE,
        scratch_shapes=[pltpu.SemaphoreType.DMA((SIDE, len(sources)))],
        cost_estimate=pl.CostEstimate(
            flops=0, bytes_accessed=SIDE * ROWS * total * 4, transcendentals=0
        ),
    )(meta, *sources)


def join_kernel(meta, *refs):
    pieces, out_ref, sems = refs[:SIDE], refs[SIDE], refs[SIDE + 1]
    width = GROUP * HD
    copies = []
    for k in range(SIDE):
        col = pl.multiple_of(((meta[0] + k) & 3) * width, width)
        copies.append(
            pltpu.make_async_copy(pieces[k], out_ref.at[:, pl.ds(col, width)], sems.at[k])
        )
    for copy in copies:
        copy.start()
    for copy in copies:
        copy.wait()


def join(meta, pieces):
    return pl.pallas_call(
        join_kernel,
        out_shape=jax.ShapeDtypeStruct((ROWS, QH * HD), jnp.bfloat16),
        in_specs=[SM] + [HB] * SIDE,
        out_specs=HB,
        scratch_shapes=[pltpu.SemaphoreType.DMA((SIDE,))],
        cost_estimate=pl.CostEstimate(flops=0, bytes_accessed=4 * MIB, transcendentals=0),
    )(meta, *pieces)


def table_kernel(meta, hf_ref, slot_ref, fill_ref, rank_ref, count_ref):
    head, line, core = meta[0], meta[1], meta[2]

    def clear(i, _):
        slot_ref[i] = 0
        fill_ref[i] = 0
        return 0

    lax.fori_loop(0, GROUPS * GROUPS, clear, 0)
    for d in range(GROUPS):
        count_ref[d] = 0

    def source(s, _):
        high, low = s // SIDE, s % SIDE
        own_head = jnp.where(core == 0, high, low)
        own_line = jnp.where(core == 0, low, high)
        base = (((line - own_line) & 3) * SIDE + ((head - own_head) & 3)) * SB
        at = s ^ meta[3]
        for b in range(SB):
            home = hf_ref[at, b]
            rank = count_ref[home]
            count_ref[home] = rank + 1
            rank_ref[at * SB + b] = rank
            slot_ref[home * GROUPS + rank] = base + b
            fill_ref[home * GROUPS + rank] = hf_ref[at, SB + b]
        return 0

    lax.fori_loop(0, GROUPS, source, 0)


def make_tables(meta, hf):
    ints = lambda n: jax.ShapeDtypeStruct((n,), jnp.int32)
    return pl.pallas_call(
        table_kernel,
        out_shape=[ints(GROUPS * GROUPS), ints(GROUPS * GROUPS), ints(GROUPS * SB)],
        in_specs=[SM, SM],
        out_specs=[SM, SM, SM],
        scratch_shapes=[pltpu.SMEM((GROUPS,), jnp.int32)],
        cost_estimate=pl.CostEstimate(flops=4096, bytes_accessed=4096, transcendentals=0),
    )(meta, hf)


def soften(scores, value_rows):
    row_max = jnp.max(scores, axis=-1, keepdims=True)
    weights = jnp.exp2((scores - row_max) * SCALE)
    totals = jnp.sum(weights, axis=-1, keepdims=True)
    mixture = jnp.dot(
        weights.astype(jnp.bfloat16), value_rows, preferred_element_type=jnp.float32
    )
    return mixture / totals


def inner(queries, key_rows):
    return lax.dot_general(
        queries, key_rows, (((1,), (1,)), ((), ())), preferred_element_type=jnp.float32
    )


def short_kernel(shifts, meta, hf_ref, slot_ref, fill_ref, rank_ref, *refs):
    count = len(shifts)
    kv_parts = refs[1 : 1 + SIDE]
    q_parts = refs[1 + SIDE : 1 + SIDE + count]
    out_parts = refs[1 + SIDE + count : 1 + SIDE + 2 * count]
    kv_ref, q_refs, out_refs, kv_sems, q_sems, out_sems = refs[-6:]
    part_rows = SIDE * ROWS
    kv_copies = [
        pltpu.make_async_copy(
            kv_parts[j], kv_ref.at[pl.ds(j * part_rows, part_rows)], kv_sems.at[j]
        )
        for j in range(SIDE)
    ]
    q_copies = [
        pltpu.make_async_copy(q_parts[n], q_refs.at[n], q_sems.at[n]) for n in range(count)
    ]
    out_copies = [
        pltpu.make_async_copy(out_refs.at[n], out_parts[n], out_sems.at[n]) for n in range(count)
    ]
    for copy in kv_copies + q_copies:
        copy.start()
    for copy in kv_copies:
        copy.wait()
    head, line, core = meta[0], meta[1], meta[2]
    width = CHUNK * BLOCK
    lane = lax.broadcasted_iota(jnp.int32, (1, width), 1)
    lane_block = lane // BLOCK
    lane_row = lane % BLOCK
    row = lax.broadcasted_iota(jnp.int32, (BLOCK, width), 0)

    for position, k in enumerate(shifts):
        q_ref, out_ref = q_refs.at[position], out_refs.at[position]
        q_copies[position].wait()
        own_head = (head - k) & 3
        own = jnp.where(core == 0, own_head * SIDE + line, line * SIDE + own_head) ^ meta[3]

        def one_block(b, _, q_ref=q_ref, out_ref=out_ref, own=own):
            home = hf_ref[own, b]
            own_fill = hf_ref[own, SB + b]
            rank = rank_ref[own * SB + b]
            first = home * GROUPS
            rows = pl.ds(pl.multiple_of(b * BLOCK, BLOCK), BLOCK)

            def attend(chunks):
                q = q_ref[rows, :]
                q = jnp.concatenate(
                    [q[:, h * HD : (h + 1) * HD] for h in range(GROUP)], axis=0
                )
                key_parts, value_parts, biases = [], [], []
                for c in range(chunks):
                    limits = []
                    for j in range(CHUNK):
                        n = c * CHUNK + j
                        start = pl.multiple_of(slot_ref[first + n] * BLOCK, BLOCK)
                        kv = kv_ref[pl.ds(start, BLOCK), :]
                        key_parts.append(kv[:, :HD])
                        value_parts.append(kv[:, HD:])
                        limits.append(jnp.where(n <= rank, fill_ref[first + n], 0))
                    limit = jnp.where(
                        lane_block < 2,
                        jnp.where(lane_block == 0, limits[0], limits[1]),
                        jnp.where(lane_block == 2, limits[2], limits[3]),
                    )
                    if c < chunks - 1:
                        bias = jnp.where(lane_row < limit, 0.0, MASKED)
                        biases.append(jnp.broadcast_to(bias, (BLOCK, width)))
                    else:
                        causal = jnp.where(
                            lane_block == rank - c * CHUNK, row + 1, BLOCK
                        )
                        limit = jnp.minimum(limit, causal)
                        biases.append(jnp.where(lane_row < limit, 0.0, MASKED))
                keys = jnp.concatenate(key_parts, axis=0)
                values = jnp.concatenate(value_parts, axis=0)
                bias = jnp.concatenate(biases, axis=1)
                scores = inner(q, keys) + jnp.concatenate([bias] * GROUP, axis=0)
                mixed = soften(scores, values)
                used = lax.broadcasted_iota(jnp.int32, (BLOCK, HD), 0) < own_fill
                for h in range(GROUP):
                    part = jnp.where(used, mixed[h * BLOCK : (h + 1) * BLOCK], 0.0)
                    out_ref[rows, h * HD : (h + 1) * HD] = part.astype(jnp.bfloat16)

            for chunks in range(1, GROUPS // CHUNK + 1):
                pl.when(rank // CHUNK == chunks - 1)(functools.partial(attend, chunks))
            return 0

        lax.fori_loop(0, SB, one_block, 0)
        out_copies[position].start()
    for copy in out_copies:
        copy.wait()


def short_attention(shifts, after, meta, hf, tables, kv_parts, q_parts):
    count = len(shifts)
    return pl.pallas_call(
        functools.partial(short_kernel, shifts),
        out_shape=[jax.ShapeDtypeStruct((ROWS, GROUP * HD), jnp.bfloat16)] * count,
        in_specs=[SM] * 5 + [HB] * (1 + SIDE + count),
        out_specs=[HB] * count,
        scratch_shapes=[
            pltpu.VMEM((GROUPS * ROWS, 2 * HD), jnp.bfloat16),
            pltpu.VMEM((count, ROWS, GROUP * HD), jnp.bfloat16),
            pltpu.VMEM((count, ROWS, GROUP * HD), jnp.bfloat16),
            pltpu.SemaphoreType.DMA((SIDE,)),
            pltpu.SemaphoreType.DMA((count,)),
            pltpu.SemaphoreType.DMA((count,)),
        ],
        compiler_params=pltpu.CompilerParams(vmem_limit_bytes=32 * MIB),
        cost_estimate=pl.CostEstimate(
            flops=count * 700_000_000, bytes_accessed=4 * MIB, transcendentals=count * 1_300_000
        ),
    )(meta, hf, *tables, after, *kv_parts, *q_parts)


def long_kernel(doc_ref, q_ref, *refs):
    out_hbm, kv_ref, query_ref, out_ref, bias_ref, sems = refs[5:]
    copies = [pltpu.make_async_copy(refs[n], kv_ref.at[n], sems.at[n]) for n in range(5)]
    copies.append(pltpu.make_async_copy(q_ref, query_ref, sems.at[5]))
    for copy in copies:
        copy.start()
    for copy in copies:
        copy.wait()
    parts = [kv_ref.at[n] for n in range(5)]
    own_doc = doc_ref[...]
    lane = lax.broadcasted_iota(jnp.int32, (LROWS, LROWS), 1)
    row = lax.broadcasted_iota(jnp.int32, (LROWS, LROWS), 0)
    for n in range(5):
        key_doc = parts[n][LROWS : LROWS + 16, :LROWS].astype(jnp.float32)[:1]
        allowed = own_doc == key_doc
        if n == 0:
            allowed = allowed & (lane <= row)
        bias_ref[:, n * LROWS : (n + 1) * LROWS] = jnp.where(allowed, 0.0, MASKED)

    def one_head(h, _):
        col = pl.multiple_of(h * HD, HD)
        vcol = pl.multiple_of((KVH + h) * HD, HD)
        keys = jnp.concatenate([p[:LROWS, pl.ds(col, HD)] for p in parts], axis=0)
        values = jnp.concatenate([p[:LROWS, pl.ds(vcol, HD)] for p in parts], axis=0)
        for i in range(GROUP):
            qcol = pl.multiple_of((h * GROUP + i) * HD, HD)
            scores = inner(query_ref[:, pl.ds(qcol, HD)], keys) + bias_ref[...]
            out_ref[:, pl.ds(qcol, HD)] = soften(scores, values).astype(jnp.bfloat16)
        return 0

    lax.fori_loop(0, KVH, one_head, 0)
    done = pltpu.make_async_copy(out_ref, out_hbm, sems.at[6])
    done.start()
    done.wait()


def long_attention(docs, queries, parts):
    return pl.pallas_call(
        long_kernel,
        out_shape=jax.ShapeDtypeStruct((LROWS, QH * HD), jnp.bfloat16),
        in_specs=[VM] + [HB] * 6,
        out_specs=HB,
        scratch_shapes=[
            pltpu.VMEM((5, LROWS + 16, 2 * KVH * HD), jnp.bfloat16),
            pltpu.VMEM((LROWS, QH * HD), jnp.bfloat16),
            pltpu.VMEM((LROWS, QH * HD), jnp.bfloat16),
            pltpu.VMEM((LROWS, 5 * LROWS), jnp.float32),
            pltpu.SemaphoreType.DMA((7,)),
        ],
        compiler_params=pltpu.CompilerParams(vmem_limit_bytes=32 * MIB),
        cost_estimate=pl.CostEstimate(
            flops=2_700_000_000, bytes_accessed=5 * MIB, transcendentals=5_200_000
        ),
    )(docs, queries, *parts)


def shards(
    short_queries,
    short_keys,
    short_values,
    block_fill,
    block_home,
    long_queries,
    long_keys,
    long_values,
    long_docs,
):
    place, rank = lax.axis_index("dp"), lax.axis_index("ctx")
    core = rank % 2
    head = jnp.where(core == 0, place // SIDE, place % SIDE)
    line = jnp.where(core == 0, place % SIDE, place // SIDE)
    meta = jnp.stack([head, line, core, place]).astype(jnp.int32)

    kv_own = split_heads(meta, short_keys.reshape(ROWS, KVH * HD), short_values.reshape(ROWS, KVH * HD))
    kv_line = [kv_own[0]] + [send(kv_own[k], along_head(k)) for k in (1, 2, 3)]
    kv_line = jnp.concatenate(kv_line, axis=0)

    q_own = split_heads(meta, short_queries.reshape(ROWS, QH * HD))
    q_parts = [q_own[0]] + [send(q_own[k], along_head(k)) for k in (1, 2, 3)]
    kv_parts = [kv_line] + [send(kv_line, along_rows(k)) for k in (1, 2, 3)]

    hf = jnp.concatenate([block_home.reshape(1, SB), block_fill.reshape(1, SB)], axis=1)
    for bit in (1, 2, 4, 8):
        hf = jnp.concatenate([hf, send(hf, other_place(bit))], axis=0)
    tables = make_tables(meta, hf)

    docs = long_docs.reshape(1, LROWS).astype(jnp.float32) + 1.0
    doc_rows = jnp.pad(docs.astype(jnp.bfloat16), ((0, 15), (0, 2 * KVH * HD - LROWS)))
    long_own = jnp.concatenate(
        [
            jnp.concatenate(
                [long_keys.reshape(LROWS, KVH * HD), long_values.reshape(LROWS, KVH * HD)], axis=1
            ),
            doc_rows,
        ],
        axis=0,
    )
    long_one = send(long_own, up_chips(1))
    long_two = send(long_own, up_chips(2))
    long_side = send(long_one, other_core)
    long_cross = send(jnp.where(core == 0, long_own, long_two), other_core)
    long_out = long_attention(
        docs.reshape(LROWS, 1),
        long_queries.reshape(LROWS, QH * HD),
        [long_own, long_one, long_two, long_side, long_cross],
    )

    back = [None] * SIDE
    for shifts in ((1, 3), (2, 0)):
        mixed = short_attention(
            shifts, long_out, meta, hf, tables, kv_parts, [q_parts[k] for k in shifts]
        )
        for k, piece in zip(shifts, mixed):
            back[k] = send(piece, along_head(-k)) if k else piece
    short_out = join(meta, back)
    return short_out.reshape(short_queries.shape), long_out.reshape(long_queries.shape)


def solution(mesh):
    return jax.shard_map(
        shards,
        mesh=mesh,
        in_specs=(
            P("dp", "ctx", None, None),
            P("dp", "ctx", None, None),
            P("dp", "ctx", None, None),
            P("dp", "ctx", None),
            P("dp", "ctx", None),
            P("dp", "ctx", None),
            P("dp", "ctx", None),
            P("dp", "ctx", None),
            P("dp", "ctx"),
        ),
        out_specs=(P("dp", "ctx", None, None), P("dp", "ctx", None)),
        check_vma=False,
    )
```

```python
import functools

import jax
import jax.numpy as jnp
from jax import lax
from jax.experimental import pallas as pl
from jax.experimental.pallas import tpu as pltpu
from jax.sharding import PartitionSpec as P

QH = 16
KVH = 4
HD = 128
BLOCK = 64
SB = 8
GROUP = QH // KVH
SIDE = 4
GROUPS = SIDE * SIDE
RANKS = 8
ROWS = SB * BLOCK
LROWS = 256
EXTRA = 16
PIECE = ROWS + EXTRA
KVW = 2 * HD
QW = GROUP * HD
CHUNK = 4
SET = 4
MASKED = -1e30
SCALE = HD**-0.5 * 1.4426950408889634
MIB = 1024 * 1024

VM = pl.BlockSpec(memory_space=pltpu.VMEM)
SM = pl.BlockSpec(memory_space=pltpu.SMEM)
HB = pl.BlockSpec(memory_space=pl.ANY)
FAR = pl.BlockSpec(memory_space=pltpu.HBM)


def pairs(step):
    found = []
    for x in range(SIDE):
        for y in range(SIDE):
            for z in range(RANKS // 2):
                for core in range(2):
                    target = step(x, y, z, core)
                    if target is not None:
                        tx, ty, tz, tcore = target
                        found.append(
                            (
                                (x * SIDE + y) * RANKS + z * 2 + core,
                                (tx * SIDE + ty) * RANKS + tz * 2 + tcore,
                            )
                        )
    return found


def send(value, step):
    return lax.ppermute(value, ("dp", "ctx"), pairs(step))


def along_head(k):
    def step(x, y, z, core):
        if core == 0:
            return (x + k) % SIDE, y, z, core
        return x, (y + k) % SIDE, z, core

    return step


def along_rows(k):
    def step(x, y, z, core):
        if core == 0:
            return x, (y + k) % SIDE, z, core
        return (x + k) % SIDE, y, z, core

    return step


def up_chips(k):
    def step(x, y, z, core):
        return (x, y, z + k, core) if z + k < RANKS // 2 else None

    return step


def other_core(x, y, z, core):
    return x, y, z, 1 - core


def where_am_i():
    place, rank = lax.axis_index("dp"), lax.axis_index("ctx")
    x, y, core = lax.shift_right_logical(place, 2), place & 3, rank & 1
    return jnp.where(core == 0, x, y), jnp.where(core == 0, y, x), core


def busy(us):
    return pl.CostEstimate(flops=int(us * 1e9), bytes_accessed=MIB, transcendentals=0)


def split_kernel(home_in, fill_in, doc_in, k_ref, v_ref, q_ref, lk_ref, lv_ref, *refs):
    outs, own, packed = refs[: SIDE - 1], refs[SIDE - 1], refs[SIDE]
    home, fill, docs, sems, few_sems = refs[SIDE + 1 :]
    mine = where_am_i()[0]
    few = [
        pltpu.make_async_copy(source, to, few_sems.at[n])
        for n, (source, to) in enumerate(((home_in, home), (fill_in, fill), (doc_in, docs)))
    ]
    copies = []
    for k in range(SIDE):
        head = (mine + k) & 3
        col = pl.multiple_of(head * HD, HD)
        out = own if k == 0 else outs[k - 1]
        moves = [(k_ref, col, HD, 0), (v_ref, col, HD, HD)]
        if k > 0:
            moves.append((q_ref, pl.multiple_of(head * QW, QW), QW, KVW))
        for n, (source, at, wide, to) in enumerate(moves):
            copies.append(
                pltpu.make_async_copy(
                    source.at[:, pl.ds(at, wide)],
                    out.at[pl.ds(0, ROWS), pl.ds(to, wide)],
                    sems.at[k, n],
                )
            )
    wide = KVH * HD
    for n, source in enumerate((lk_ref, lv_ref)):
        to = packed.at[pl.ds(0, LROWS), pl.ds(n * wide, wide)]
        copies.append(pltpu.make_async_copy(source, to, sems.at[SIDE, n]))
    for copy in few + copies:
        copy.start()
    for copy in few:
        copy.wait()
    row = lax.broadcasted_iota(jnp.int32, (EXTRA, KVW), 0)
    facts = jnp.zeros((EXTRA, KVW), jnp.int32)
    for b in range(SB):
        facts = jnp.where(row == b, home[b], facts)
        facts = jnp.where(row == SB + b, fill[b], facts)
    facts = facts.astype(jnp.float32).astype(jnp.bfloat16)
    own[ROWS:, :] = facts
    for out in outs:
        out[ROWS:, :KVW] = facts
        out[ROWS:, KVW:] = jnp.zeros((EXTRA, QW), jnp.bfloat16)
    doc_row = docs[...].astype(jnp.float32) + 1.0
    packed[LROWS:, :LROWS] = jnp.broadcast_to(doc_row, (EXTRA, LROWS)).astype(jnp.bfloat16)
    packed[LROWS:, LROWS:] = jnp.zeros((EXTRA, 2 * wide - LROWS), jnp.bfloat16)
    for copy in copies:
        copy.wait()


def split(home, fill, docs, keys, values, queries, long_keys, long_values):
    shapes = [jax.ShapeDtypeStruct((PIECE, KVW + QW), jnp.bfloat16)] * (SIDE - 1)
    shapes += [
        jax.ShapeDtypeStruct((PIECE, KVW), jnp.bfloat16),
        jax.ShapeDtypeStruct((LROWS + EXTRA, 2 * KVH * HD), jnp.bfloat16),
    ]
    return pl.pallas_call(
        split_kernel,
        out_shape=shapes,
        in_specs=[FAR] * 8,
        out_specs=[VM] * (SIDE + 1),
        scratch_shapes=[
            pltpu.SMEM((SB,), jnp.int32),
            pltpu.SMEM((SB,), jnp.int32),
            pltpu.VMEM((1, LROWS), jnp.int32),
            pltpu.SemaphoreType.DMA((SIDE + 1, 3)),
            pltpu.SemaphoreType.DMA((3,)),
        ],
        compiler_params=pltpu.CompilerParams(vmem_limit_bytes=60 * MIB),
        cost_estimate=busy(2),
    )(home, fill, docs, keys, values, queries, long_keys, long_values)


def stack_kernel(*refs):
    for n in range(SIDE):
        refs[-1][n * PIECE : (n + 1) * PIECE] = refs[n][:, :KVW]


def stack(pieces):
    return pl.pallas_call(
        stack_kernel,
        out_shape=jax.ShapeDtypeStruct((SIDE * PIECE, KVW), jnp.bfloat16),
        in_specs=[VM] * SIDE,
        out_specs=VM,
        compiler_params=pltpu.CompilerParams(vmem_limit_bytes=2 * MIB),
        cost_estimate=busy(1),
    )(*pieces)


def join_kernel(*refs):
    pieces, out_ref, sems = refs[:SIDE], refs[SIDE], refs[SIDE + 1]
    mine = where_am_i()[0]
    copies = []
    for k in range(SIDE):
        col = pl.multiple_of(((mine + k) & 3) * QW, QW)
        copies.append(
            pltpu.make_async_copy(pieces[k], out_ref.at[:, pl.ds(col, QW)], sems.at[k])
        )
    for copy in copies:
        copy.start()
    for copy in copies:
        copy.wait()


def join(pieces):
    return pl.pallas_call(
        join_kernel,
        out_shape=jax.ShapeDtypeStruct((ROWS, QH * HD), jnp.bfloat16),
        in_specs=[VM] * SIDE,
        out_specs=FAR,
        scratch_shapes=[pltpu.SemaphoreType.DMA((SIDE,))],
        compiler_params=pltpu.CompilerParams(vmem_limit_bytes=MIB),
        cost_estimate=busy(2),
    )(*pieces)


def fill_table(kv_ref, table_ref):
    head, line, core = where_am_i()
    shape = (GROUPS, HD)
    lane = lax.broadcasted_iota(jnp.int32, shape, 1)
    row = lax.broadcasted_iota(jnp.int32, shape, 0)
    facts = jnp.full(shape, -1.0, jnp.float32)
    for p in range(GROUPS):
        piece = kv_ref[p * PIECE + ROWS : (p + 1) * PIECE, :HD].astype(jnp.float32)
        facts = jnp.where(lane == p, piece, facts)
    facts = facts.astype(jnp.int32)

    def order(p):
        own_head = (head - p) & 3
        own_line = (line - lax.shift_right_logical(p, 2)) & 3
        return jnp.where(core == 0, own_head * SIDE + own_line, own_line * SIDE + own_head)

    one = lax.broadcasted_iota(jnp.int32, (HD, HD), 0)
    two = lax.broadcasted_iota(jnp.int32, (HD, HD), 1)
    earlier = jnp.where((order(one) < order(two)) & (one < GROUPS), 1.0, 0.0)
    here = jnp.zeros(shape, jnp.float32)
    slots = jnp.zeros(shape, jnp.int32)
    fills = jnp.zeros(shape, jnp.int32)
    for b in range(SB):
        same = facts[b : b + 1] == row
        here = jnp.where(same, 1.0, here)
        slots = jnp.where(same, lane * (PIECE // EXTRA) + b * (BLOCK // EXTRA), slots)
        fills = jnp.where(same, facts[SB + b : SB + b + 1], fills)
    ranks = jnp.dot(here, earlier, preferred_element_type=jnp.float32).astype(jnp.int32)
    own_rows = lax.broadcasted_iota(jnp.int32, (SB, HD), 0)
    own_ranks = jnp.zeros((SB, HD), jnp.int32)
    for d in range(GROUPS):
        own_ranks = jnp.where(facts[:SB] == d, ranks[d : d + 1], own_ranks)
    place = jnp.zeros((SB, HD), jnp.int32)
    for b in range(SB):
        other = own_ranks[b : b + 1]
        ahead = (other > own_ranks) | ((other == own_ranks) & (own_rows > b))
        place = place + jnp.where(ahead, 1, 0)
    listed = [jnp.zeros((SB, HD), jnp.int32) for _ in range(4)]
    for b in range(SB):
        chosen = place[b : b + 1] == own_rows
        found = (b, facts[b : b + 1], facts[SB + b : SB + b + 1], own_ranks[b : b + 1])
        listed = [jnp.where(chosen, new, old) for new, old in zip(found, listed)]
    for n in range(4):
        table_ref[n * SB : (n + 1) * SB] = listed[n]
    ranks = jnp.where(here > 0.0, ranks, -1)
    slot_list = jnp.zeros(shape, jnp.int32)
    fill_list = jnp.zeros(shape, jnp.int32)
    for r in range(GROUPS):
        chosen = ranks == r
        slot = jnp.sum(jnp.where(chosen, slots, 0), axis=1, keepdims=True)
        fill = jnp.sum(jnp.where(chosen, fills, 0), axis=1, keepdims=True)
        slot_list = jnp.where(lane == r, slot, slot_list)
        fill_list = jnp.where(lane == r, fill, fill_list)
    table_ref[4 * SB : 4 * SB + GROUPS] = slot_list
    table_ref[4 * SB + GROUPS :] = fill_list


def soften(scores, value_rows):
    row_max = jnp.max(scores, axis=-1, keepdims=True)
    weights = jnp.exp2((scores - row_max) * SCALE)
    totals = jnp.sum(weights, axis=-1, keepdims=True)
    mixture = jnp.dot(
        weights.astype(jnp.bfloat16), value_rows, preferred_element_type=jnp.float32
    )
    return mixture / totals


def inner(queries, key_rows):
    return lax.dot_general(
        queries, key_rows, (((1,), (1,)), ((), ())), preferred_element_type=jnp.float32
    )


def short_kernel(shifts, first, waits, q_all, *refs):
    count = len(shifts)
    line_parts, kv_parts = refs[: SIDE - 1], refs[SIDE - 1 : 2 * SIDE - 1]
    refs = refs[2 * SIDE - 1 + waits :]
    if first:
        out_parts, table = refs[:count], refs[count]
        table_ref, table_sem = refs[-2:]
        refs = refs[count + 1 :]
    else:
        table, out_parts = refs[0], refs[1 : 1 + count]
        refs = refs[1 + count :]
    kv_ref, q_ref, out_ref, mix_ref, top_ref, kv_sems, q_sems = refs[:7]
    col = pl.multiple_of(where_am_i()[0] * QW, QW)
    wanted = [
        line_parts[k - 1].at[pl.ds(0, ROWS), pl.ds(KVW, QW)] if k else q_all.at[:, pl.ds(col, QW)]
        for k in shifts
    ]
    part_rows = SIDE * PIECE
    copies = [
        pltpu.make_async_copy(
            kv_parts[n], kv_ref.at[pl.ds(n * part_rows, part_rows)], kv_sems.at[n]
        )
        for n in range(SIDE)
    ]
    copies += [
        pltpu.make_async_copy(source, q_ref.at[pl.ds(n * ROWS, ROWS)], q_sems.at[n])
        for n, source in enumerate(wanted)
    ]
    for copy in copies:
        copy.start()
    for copy in copies:
        copy.wait()
    if first:
        fill_table(kv_ref, table_ref)
        table_copy = pltpu.make_async_copy(table_ref, table, table_sem)
        table_copy.start()
        table_copy.wait()
    width = CHUNK * BLOCK
    lane = lax.broadcasted_iota(jnp.int32, (BLOCK, width), 1)
    lane_block = lane // BLOCK
    lane_row = lane % BLOCK
    row = lax.broadcasted_iota(jnp.int32, (BLOCK, width), 0)
    ones = jnp.ones((width, HD), jnp.bfloat16)

    def one_set(t, _):
        piece = t // (SB // SET)
        k = piece + shifts[0]
        base = (t % (SB // SET)) * SET

        def fact(n, u):
            return table[n * SB + base + u, k]

        def rows_of(u):
            return pl.ds(pl.multiple_of(piece * ROWS + fact(0, u) * BLOCK, BLOCK), BLOCK)

        def scores_of(u, c):
            home, rank = fact(1, u), fact(3, u)
            q = q_ref[rows_of(u), :]
            q = jnp.concatenate([q[:, h * HD : (h + 1) * HD] for h in range(GROUP)], axis=0)
            limits, keys, values = [], [], []
            for j in range(CHUNK):
                n = c * CHUNK + j
                start = pl.multiple_of(table[4 * SB + home, n] * EXTRA, EXTRA)
                kv = kv_ref[pl.ds(start, BLOCK), :]
                keys.append(kv[:, :HD])
                values.append(kv[:, HD:])
                limits.append(jnp.where(n <= rank, table[4 * SB + GROUPS + home, n], 0))
            limit = jnp.where(
                lane_block < 2,
                jnp.where(lane_block == 0, limits[0], limits[1]),
                jnp.where(lane_block == 2, limits[2], limits[3]),
            )
            causal = jnp.where(lane_block == rank - c * CHUNK, row + 1, BLOCK)
            bias = jnp.where(lane_row < jnp.minimum(limit, causal), 0.0, MASKED)
            scores = inner(q, jnp.concatenate(keys, axis=0))
            scores = scores + jnp.concatenate([bias] * GROUP, axis=0)
            values = jnp.concatenate([jnp.concatenate(values, axis=0), ones], axis=1)
            return scores, values

        def weigh(scores, top, values):
            weights = jnp.exp2((scores - top) * SCALE).astype(jnp.bfloat16)
            return jnp.dot(weights, values, preferred_element_type=jnp.float32)

        for u in range(SET):
            scores, values = scores_of(u, 0)
            top = jnp.max(scores, axis=-1, keepdims=True)
            top_ref[u] = jnp.broadcast_to(top, (GROUP * BLOCK, HD))
            mix_ref[u] = weigh(scores, top, values)

        def later(c, _):
            for u in range(SET):
                scores, values = scores_of(u, c)
                old = top_ref[u]
                top = jnp.broadcast_to(jnp.max(scores, axis=-1, keepdims=True), old.shape)
                top = jnp.maximum(old, top)
                top_ref[u] = top
                shrink = jnp.exp2((old - top) * SCALE)
                shrink = jnp.concatenate([shrink, shrink], axis=1)
                mix_ref[u] = mix_ref[u] * shrink + weigh(scores, jnp.concatenate([top, top], axis=1), values)
            return 0

        lax.fori_loop(1, fact(3, 0) // CHUNK + 1, later, 0)
        for u in range(SET):
            mixed = mix_ref[u]
            mixed = mixed[:, :HD] / mixed[:, HD:]
            used = row[:, :HD] < fact(2, u)
            for h in range(GROUP):
                part = jnp.where(used, mixed[h * BLOCK : (h + 1) * BLOCK], 0.0)
                out_ref[rows_of(u), h * HD : (h + 1) * HD] = part.astype(jnp.bfloat16)
        return 0

    lax.fori_loop(0, count * (SB // SET), one_set, 0)
    for n in range(count):
        out_parts[n][...] = out_ref[n * ROWS : (n + 1) * ROWS]


def short_attention(shifts, table, after, queries, line_parts, kv_parts):
    count = len(shifts)
    first = table is None
    outs = [jax.ShapeDtypeStruct((ROWS, QW), jnp.bfloat16)] * count
    scratch = [
        pltpu.VMEM((GROUPS * PIECE, KVW), jnp.bfloat16),
        pltpu.VMEM((count * ROWS, QW), jnp.bfloat16),
        pltpu.VMEM((count * ROWS, QW), jnp.bfloat16),
        pltpu.VMEM((SET, GROUP * BLOCK, 2 * HD), jnp.float32),
        pltpu.VMEM((SET, GROUP * BLOCK, HD), jnp.float32),
        pltpu.SemaphoreType.DMA((SIDE,)),
        pltpu.SemaphoreType.DMA((count,)),
    ]
    if first:
        outs = outs + [jax.ShapeDtypeStruct((4 * GROUPS, HD), jnp.int32)]
        scratch += [pltpu.VMEM((4 * GROUPS, HD), jnp.int32), pltpu.SemaphoreType.DMA(())]
    found = pl.pallas_call(
        functools.partial(short_kernel, shifts, first, len(after)),
        out_shape=outs,
        in_specs=[FAR]
        + [HB] * (2 * SIDE - 1)
        + [SM if first else HB] * len(after)
        + ([] if first else [SM]),
        out_specs=[VM] * count + ([SM] if first else []),
        scratch_shapes=scratch,
        compiler_params=pltpu.CompilerParams(vmem_limit_bytes=24 * MIB),
        cost_estimate=busy(4 * count),
    )(queries, *line_parts, *kv_parts, *after, *([] if first else [table]))
    return (found[:count], found[count]) if first else (found, table)


def long_kernel(q_in, *refs):
    parts = refs[:5]
    out_ref, token, q_ref, bias_ref, sem = refs[5:]
    copy = pltpu.make_async_copy(q_in, q_ref, sem)
    copy.start()
    token[0] = 0
    square = (LROWS, LROWS)
    lane = lax.broadcasted_iota(jnp.int32, square, 1)
    row = lax.broadcasted_iota(jnp.int32, square, 0)
    docs = [p[LROWS : LROWS + EXTRA, :LROWS].astype(jnp.float32)[:1] for p in parts]
    own_doc = jnp.transpose(jnp.broadcast_to(docs[0], square))
    for n in range(5):
        allowed = own_doc == docs[n]
        if n == 0:
            allowed = allowed & (lane <= row)
        bias_ref[:, n * LROWS : (n + 1) * LROWS] = jnp.where(allowed, 0.0, MASKED)
    copy.wait()

    def one_head(h, _):
        col = pl.multiple_of(h * HD, HD)
        vcol = pl.multiple_of((KVH + h) * HD, HD)
        keys = jnp.concatenate([p[:LROWS, pl.ds(col, HD)] for p in parts], axis=0)
        values = jnp.concatenate([p[:LROWS, pl.ds(vcol, HD)] for p in parts], axis=0)
        for i in range(GROUP):
            qcol = pl.multiple_of((h * GROUP + i) * HD, HD)
            scores = inner(q_ref[:, pl.ds(qcol, HD)], keys) + bias_ref[...]
            out_ref[:, pl.ds(qcol, HD)] = soften(scores, values).astype(jnp.bfloat16)
        return 0

    lax.fori_loop(0, KVH, one_head, 0)


def long_attention(queries, parts):
    return pl.pallas_call(
        long_kernel,
        out_shape=[
            jax.ShapeDtypeStruct((LROWS, QH * HD), jnp.bfloat16),
            jax.ShapeDtypeStruct((1,), jnp.int32),
        ],
        in_specs=[FAR] + [VM] * 5,
        out_specs=[VM, SM],
        scratch_shapes=[
            pltpu.VMEM((LROWS, QH * HD), jnp.bfloat16),
            pltpu.VMEM((LROWS, 5 * LROWS), jnp.float32),
            pltpu.SemaphoreType.DMA(()),
        ],
        compiler_params=pltpu.CompilerParams(vmem_limit_bytes=20 * MIB),
        cost_estimate=busy(0.1),
    )(queries, *parts)


def shards(
    short_queries,
    short_keys,
    short_values,
    block_fill,
    block_home,
    long_queries,
    long_keys,
    long_values,
    long_docs,
):
    queries = short_queries.reshape(ROWS, QH * HD)
    *own, own_kv, packed = split(
        block_home.reshape(SB),
        block_fill.reshape(SB),
        long_docs.reshape(1, LROWS),
        short_keys.reshape(ROWS, KVH * HD),
        short_values.reshape(ROWS, KVH * HD),
        queries,
        long_keys.reshape(LROWS, KVH * HD),
        long_values.reshape(LROWS, KVH * HD),
    )
    line_parts = [send(own[k - 1], along_head(k)) for k in (1, 2, 3)]
    long_one = send(packed, up_chips(1))
    long_two = send(packed, up_chips(2))
    stacked = stack([own_kv] + line_parts)
    kv_parts = [stacked] + [send(stacked, along_rows(k)) for k in (1, 2, 3)]
    long_side = send(long_one, other_core)
    core = lax.axis_index("ctx") % 2
    long_cross = send(jnp.where(core == 0, packed, long_two), other_core)
    long_out, token = long_attention(
        long_queries.reshape(LROWS, QH * HD),
        [packed, long_one, long_two, long_side, long_cross],
    )

    mixed, table = short_attention((1, 2, 3), None, [token], queries, line_parts, kv_parts)
    back = [send(piece, along_head(-k)) for k, piece in zip((1, 2, 3), mixed)]
    kept, _ = short_attention((0,), table, [], queries, line_parts, kv_parts)
    short_out = join([kept[0]] + back)
    return short_out.reshape(short_queries.shape), long_out.reshape(long_queries.shape)


def solution(mesh):
    return jax.shard_map(
        shards,
        mesh=mesh,
        in_specs=(
            P("dp", "ctx", None, None),
            P("dp", "ctx", None, None),
            P("dp", "ctx", None, None),
            P("dp", "ctx", None),
            P("dp", "ctx", None),
            P("dp", "ctx", None),
            P("dp", "ctx", None),
            P("dp", "ctx", None),
            P("dp", "ctx"),
        ),
        out_specs=(P("dp", "ctx", None, None), P("dp", "ctx", None)),
        check_vma=False,
    )
```

```python
import functools

import jax
import jax.numpy as jnp
from jax import lax
from jax.experimental import pallas as pl
from jax.experimental.pallas import tpu as pltpu
from jax.sharding import PartitionSpec as P

QH = 16
KVH = 4
HD = 128
BLOCK = 64
SB = 8
GROUP = QH // KVH
SIDE = 4
GROUPS = SIDE * SIDE
RANKS = 8
ROWS = SB * BLOCK
LROWS = 256
EXTRA = 16
PIECE = ROWS + EXTRA
KVW = 2 * HD
QW = GROUP * HD
CHUNK = 4
SET = 4
ORDER = (2, 1, 3)
WIDE = 2 * CHUNK
MASKED = -1e30
SCALE = HD**-0.5 * 1.4426950408889634
MIB = 1024 * 1024

VM = pl.BlockSpec(memory_space=pltpu.VMEM)
SM = pl.BlockSpec(memory_space=pltpu.SMEM)
HB = pl.BlockSpec(memory_space=pl.ANY)
FAR = pl.BlockSpec(memory_space=pltpu.HBM)


def pairs(step):
    found = []
    for x in range(SIDE):
        for y in range(SIDE):
            for z in range(RANKS // 2):
                for core in range(2):
                    target = step(x, y, z, core)
                    if target is not None:
                        tx, ty, tz, tcore = target
                        found.append(
                            (
                                (x * SIDE + y) * RANKS + z * 2 + core,
                                (tx * SIDE + ty) * RANKS + tz * 2 + tcore,
                            )
                        )
    return found


def send(value, step):
    return lax.ppermute(value, ("dp", "ctx"), pairs(step))


def along_head(k):
    def step(x, y, z, core):
        if core == 0:
            return (x + k) % SIDE, y, z, core
        return x, (y + k) % SIDE, z, core

    return step


def along_rows(k):
    def step(x, y, z, core):
        if core == 0:
            return x, (y + k) % SIDE, z, core
        return (x + k) % SIDE, y, z, core

    return step


def up_chips(k):
    def step(x, y, z, core):
        return (x, y, z + k, core) if z + k < RANKS // 2 else None

    return step


def other_core(x, y, z, core):
    return x, y, z, 1 - core


def where_am_i():
    place, rank = lax.axis_index("dp"), lax.axis_index("ctx")
    x, y, core = lax.shift_right_logical(place, 2), place & 3, rank & 1
    return jnp.where(core == 0, x, y), jnp.where(core == 0, y, x), core


def busy(us):
    return pl.CostEstimate(flops=int(us * 1e9), bytes_accessed=MIB, transcendentals=0)


def split_kernel(home_in, fill_in, doc_in, k_ref, v_ref, q_ref, lk_ref, lv_ref, *refs):
    outs, packed_out = refs[: SIDE + 1], refs[SIDE + 1]
    refs = refs[SIDE + 2 :]
    home, fill, docs, pieces, own_q, packed, sems, few_sems, out_sems = refs
    mine = where_am_i()[0]
    few = [
        pltpu.make_async_copy(source, to, few_sems.at[n])
        for n, (source, to) in enumerate(((home_in, home), (fill_in, fill), (doc_in, docs)))
    ]
    for copy in few:
        copy.start()
    copies = {}
    for k in ORDER + (0,):
        head = (mine + k) & 3
        col = pl.multiple_of(head * HD, HD)
        qcol = pl.multiple_of(head * QW, QW)
        piece = pieces.at[k]
        goals = [
            (k_ref.at[:, pl.ds(col, HD)], piece.at[pl.ds(0, ROWS), pl.ds(0, HD)]),
            (v_ref.at[:, pl.ds(col, HD)], piece.at[pl.ds(0, ROWS), pl.ds(HD, HD)]),
            (
                q_ref.at[:, pl.ds(qcol, QW)],
                piece.at[pl.ds(0, ROWS), pl.ds(KVW, QW)] if k else own_q,
            ),
        ]
        copies[k] = [
            pltpu.make_async_copy(source, to, sems.at[k, n]) for n, (source, to) in enumerate(goals)
        ]
        for copy in copies[k]:
            copy.start()
    wide = KVH * HD
    long_copies = [
        pltpu.make_async_copy(
            source, packed.at[pl.ds(0, LROWS), pl.ds(n * wide, wide)], sems.at[SIDE, n]
        )
        for n, source in enumerate((lk_ref, lv_ref))
    ]
    for copy in long_copies:
        copy.start()
    for copy in few:
        copy.wait()
    row = lax.broadcasted_iota(jnp.int32, (EXTRA, KVW), 0)
    facts = jnp.zeros((EXTRA, KVW), jnp.int32)
    for b in range(SB):
        facts = jnp.where(row == b, home[b], facts)
        facts = jnp.where(row == SB + b, fill[b], facts)
    facts = facts.astype(jnp.float32).astype(jnp.bfloat16)
    for k in range(SIDE):
        pieces[k, ROWS:, :KVW] = facts
        if k:
            pieces[k, ROWS:, KVW:] = jnp.zeros((EXTRA, QW), jnp.bfloat16)
    doc_row = docs[...].astype(jnp.float32) + 1.0
    packed[LROWS:, :LROWS] = jnp.broadcast_to(doc_row, (EXTRA, LROWS)).astype(jnp.bfloat16)
    packed[LROWS:, LROWS:] = jnp.zeros((EXTRA, 2 * wide - LROWS), jnp.bfloat16)
    done = []
    for k in ORDER + (0,):
        for copy in copies[k]:
            copy.wait()
        source = pieces.at[k] if k else pieces.at[0, :, pl.ds(0, KVW)]
        done.append(pltpu.make_async_copy(source, outs[k], out_sems.at[k]))
        done[-1].start()
    done.append(pltpu.make_async_copy(own_q, outs[SIDE], out_sems.at[SIDE]))
    done[-1].start()
    for copy in long_copies:
        copy.wait()
    done.append(pltpu.make_async_copy(packed, packed_out, out_sems.at[SIDE + 1]))
    done[-1].start()
    for copy in done:
        copy.wait()


def split(home, fill, docs, keys, values, queries, long_keys, long_values):
    shapes = [(PIECE, KVW)] + [(PIECE, KVW + QW)] * (SIDE - 1)
    shapes += [(ROWS, QW), (LROWS + EXTRA, 2 * KVH * HD)]
    return pl.pallas_call(
        split_kernel,
        out_shape=[jax.ShapeDtypeStruct(shape, jnp.bfloat16) for shape in shapes],
        in_specs=[FAR] * 8,
        out_specs=[FAR] * (SIDE + 2),
        scratch_shapes=[
            pltpu.SMEM((SB,), jnp.int32),
            pltpu.SMEM((SB,), jnp.int32),
            pltpu.VMEM((1, LROWS), jnp.int32),
            pltpu.VMEM((SIDE, PIECE, KVW + QW), jnp.bfloat16),
            pltpu.VMEM((ROWS, QW), jnp.bfloat16),
            pltpu.VMEM((LROWS + EXTRA, 2 * KVH * HD), jnp.bfloat16),
            pltpu.SemaphoreType.DMA((SIDE + 1, 3)),
            pltpu.SemaphoreType.DMA((3,)),
            pltpu.SemaphoreType.DMA((SIDE + 2,)),
        ],
        compiler_params=pltpu.CompilerParams(vmem_limit_bytes=60 * MIB),
        cost_estimate=busy(2),
    )(home, fill, docs, keys, values, queries, long_keys, long_values)


def stack_kernel(*refs):
    for n in range(SIDE):
        refs[-1][n * PIECE : (n + 1) * PIECE] = refs[n][:, :KVW]


def stack(pieces):
    return pl.pallas_call(
        stack_kernel,
        out_shape=jax.ShapeDtypeStruct((SIDE * PIECE, KVW), jnp.bfloat16),
        in_specs=[VM] * SIDE,
        out_specs=VM,
        compiler_params=pltpu.CompilerParams(vmem_limit_bytes=2 * MIB),
        cost_estimate=busy(1),
    )(*pieces)


def join_kernel(*refs):
    pieces, out_ref, sems = refs[:SIDE], refs[SIDE], refs[SIDE + 1]
    mine = where_am_i()[0]
    copies = []
    for k in range(SIDE):
        col = pl.multiple_of(((mine + k) & 3) * QW, QW)
        copies.append(
            pltpu.make_async_copy(pieces[k], out_ref.at[:, pl.ds(col, QW)], sems.at[k])
        )
    for copy in copies:
        copy.start()
    for copy in copies:
        copy.wait()


def join(pieces):
    return pl.pallas_call(
        join_kernel,
        out_shape=jax.ShapeDtypeStruct((ROWS, QH * HD), jnp.bfloat16),
        in_specs=[VM] * SIDE,
        out_specs=FAR,
        scratch_shapes=[pltpu.SemaphoreType.DMA((SIDE,))],
        compiler_params=pltpu.CompilerParams(vmem_limit_bytes=MIB),
        cost_estimate=busy(2),
    )(*pieces)


def fill_table(kv_ref, table_ref):
    head, line, core = where_am_i()
    shape = (GROUPS, HD)
    lane = lax.broadcasted_iota(jnp.int32, shape, 1)
    row = lax.broadcasted_iota(jnp.int32, shape, 0)
    facts = jnp.full(shape, -1.0, jnp.float32)
    for p in range(GROUPS):
        piece = kv_ref[p * PIECE + ROWS : (p + 1) * PIECE, :HD].astype(jnp.float32)
        facts = jnp.where(lane == p, piece, facts)
    facts = facts.astype(jnp.int32)

    def order(p):
        own_head = (head - p) & 3
        own_line = (line - lax.shift_right_logical(p, 2)) & 3
        return jnp.where(core == 0, own_head * SIDE + own_line, own_line * SIDE + own_head)

    one = lax.broadcasted_iota(jnp.int32, (HD, HD), 0)
    two = lax.broadcasted_iota(jnp.int32, (HD, HD), 1)
    earlier = jnp.where((order(one) < order(two)) & (one < GROUPS), 1.0, 0.0)
    here = jnp.zeros(shape, jnp.float32)
    slots = jnp.zeros(shape, jnp.int32)
    fills = jnp.zeros(shape, jnp.int32)
    for b in range(SB):
        same = facts[b : b + 1] == row
        here = jnp.where(same, 1.0, here)
        slots = jnp.where(same, lane * (PIECE // EXTRA) + b * (BLOCK // EXTRA), slots)
        fills = jnp.where(same, facts[SB + b : SB + b + 1], fills)
    ranks = jnp.dot(here, earlier, preferred_element_type=jnp.float32).astype(jnp.int32)
    own_ranks = jnp.zeros((SB, HD), jnp.int32)
    for d in range(GROUPS):
        own_ranks = jnp.where(facts[:SB] == d, ranks[d : d + 1], own_ranks)
    table_ref[: 2 * SB] = facts
    table_ref[2 * SB : 3 * SB] = own_ranks
    table_ref[3 * SB : 4 * SB] = own_ranks
    ranks = jnp.where(here > 0.0, ranks, -1)
    slot_list = jnp.zeros(shape, jnp.int32)
    fill_list = jnp.zeros(shape, jnp.int32)
    for r in range(GROUPS):
        chosen = ranks == r
        slot = jnp.sum(jnp.where(chosen, slots, 0), axis=1, keepdims=True)
        fill = jnp.sum(jnp.where(chosen, fills, 0), axis=1, keepdims=True)
        slot_list = jnp.where(lane == r, slot, slot_list)
        fill_list = jnp.where(lane == r, fill, fill_list)
    table_ref[4 * SB : 4 * SB + GROUPS] = slot_list
    table_ref[4 * SB + GROUPS :] = fill_list


def soften(scores, value_rows):
    row_max = jnp.max(scores, axis=-1, keepdims=True)
    weights = jnp.exp2((scores - row_max) * SCALE)
    totals = jnp.sum(weights, axis=-1, keepdims=True)
    mixture = jnp.dot(
        weights.astype(jnp.bfloat16), value_rows, preferred_element_type=jnp.float32
    )
    return mixture / totals


def inner(queries, key_rows):
    return lax.dot_general(
        queries, key_rows, (((1,), (1,)), ((), ())), preferred_element_type=jnp.float32
    )


def short_kernel(shifts, first, waits, *refs):
    count = len(shifts)
    q_parts, kv_parts = refs[:count], refs[count : count + SIDE]
    refs = refs[count + SIDE + waits :]
    if first:
        out_parts, table = refs[:count], refs[count]
        table_ref, table_sem = refs[-2:]
        refs = refs[count + 1 :]
    else:
        table, out_parts = refs[0], refs[1 : 1 + count]
        refs = refs[1 + count :]
    kv_ref, q_ref, out_ref, mix_ref, top_ref, list_ref, kv_sems, q_sems = refs[:8]
    part_rows = SIDE * PIECE
    copies = [
        pltpu.make_async_copy(
            kv_parts[n], kv_ref.at[pl.ds(n * part_rows, part_rows)], kv_sems.at[n]
        )
        for n in range(SIDE)
    ]
    copies += [
        pltpu.make_async_copy(
            q_parts[n].at[pl.ds(0, ROWS), pl.ds(KVW if k else 0, QW)],
            q_ref.at[pl.ds(n * ROWS, ROWS)],
            q_sems.at[n],
        )
        for n, k in enumerate(shifts)
    ]
    for copy in copies:
        copy.start()
    for copy in copies:
        copy.wait()
    if first:
        fill_table(kv_ref, table_ref)
        table_copy = pltpu.make_async_copy(table_ref, table, table_sem)
        table_copy.start()
        table_copy.wait()
    low = lax.broadcasted_iota(jnp.int32, (BLOCK, HD), 1) < BLOCK
    lane_row = lax.broadcasted_iota(jnp.int32, (BLOCK, HD), 1) % BLOCK
    row = lax.broadcasted_iota(jnp.int32, (BLOCK, HD), 0)

    total = count * SB
    over = [0, 0, 0]
    ranks = []
    for n in range(total):
        rank = table[2 * SB + n % SB, shifts[0] + n // SB]
        ranks.append(rank)
        over = [old + jnp.where(rank >= 4 * (i + 1), 1, 0) for i, old in enumerate(over)]
    spots = [over[0], over[1], over[2], 0]
    for n in range(total):
        b, k = n % SB, shifts[0] + n // SB
        level = lax.shift_right_logical(ranks[n], 2)
        spot = jnp.where(
            level < 2,
            jnp.where(level == 0, spots[0], spots[1]),
            jnp.where(level == 2, spots[2], spots[3]),
        )
        list_ref[0, spot] = n
        list_ref[1, spot] = table[b, k]
        list_ref[2, spot] = ranks[n]
        list_ref[3, spot] = table[SB + b, k]
        spots = [old + jnp.where(level == i, 1, 0) for i, old in enumerate(spots)]

    def rows_of(at):
        return pl.ds(pl.multiple_of(list_ref[0, at] * BLOCK, BLOCK), BLOCK)

    def scores_of(at, first_key, blocks):
        home, rank = list_ref[1, at], list_ref[2, at]
        q = q_ref[rows_of(at), :]
        q = jnp.concatenate([q[:, h * HD : (h + 1) * HD] for h in range(GROUP)], axis=0)
        fills, shifts_in, keys, values, biases = [], [], [], [], []
        for j in range(blocks):
            n = first_key + j
            start = pl.multiple_of(table[4 * SB + home, n] * EXTRA, EXTRA)
            kv = kv_ref[pl.ds(start, BLOCK), :]
            keys.append(kv[:, :HD])
            values.append(kv[:, HD:])
            fills.append(jnp.where(n <= rank, table[4 * SB + GROUPS + home, n], 0))
            shifts_in.append(jnp.where(n == rank, 1, BLOCK))
        for j in range(0, blocks, 2):
            limit = jnp.minimum(
                jnp.where(low, fills[j], fills[j + 1]),
                row + jnp.where(low, shifts_in[j], shifts_in[j + 1]),
            )
            biases.append(jnp.where(lane_row < limit, 0.0, MASKED))
        scores = inner(q, jnp.concatenate(keys, axis=0))
        scores = scores + jnp.concatenate([jnp.concatenate(biases, axis=1)] * GROUP, axis=0)
        ones = jnp.ones((blocks * BLOCK, HD), jnp.bfloat16)
        return scores, jnp.concatenate([jnp.concatenate(values, axis=0), ones], axis=1)

    def weigh(scores, top, values):
        weights = jnp.exp2((scores - top) * SCALE).astype(jnp.bfloat16)
        return jnp.dot(weights, values, preferred_element_type=jnp.float32)

    def finish(at, mixed):
        mixed = mixed[:, :HD] / mixed[:, HD:]
        used = row < list_ref[3, at]
        for h in range(GROUP):
            part = jnp.where(used, mixed[h * BLOCK : (h + 1) * BLOCK], 0.0)
            out_ref[rows_of(at), h * HD : (h + 1) * HD] = part.astype(jnp.bfloat16)

    def in_one(blocks):
        def body(t, _):
            for u in range(SET):
                at = t * SET + u
                scores, values = scores_of(at, 0, blocks)
                top = jnp.max(scores, axis=-1, keepdims=True)
                finish(at, weigh(scores, top, values))
            return 0

        return body

    def in_two(t, _):
        for u in range(SET):
            scores, values = scores_of(t * SET + u, 0, WIDE)
            top = jnp.max(scores, axis=-1, keepdims=True)
            top_ref[u] = jnp.broadcast_to(top, (GROUP * BLOCK, HD))
            mix_ref[u] = weigh(scores, top, values)
        for u in range(SET):
            scores, values = scores_of(t * SET + u, WIDE, WIDE)
            old = top_ref[u]
            top = jnp.broadcast_to(jnp.max(scores, axis=-1, keepdims=True), old.shape)
            top = jnp.maximum(old, top)
            shrink = jnp.exp2((old - top) * SCALE)
            shrink = jnp.concatenate([shrink, shrink], axis=1)
            top = jnp.concatenate([top] * (WIDE // 2), axis=1)
            finish(t * SET + u, mix_ref[u] * shrink + weigh(scores, top, values))
        return 0

    twice = (over[1] + SET - 1) // SET
    once = (over[0] + SET - 1) // SET
    lax.fori_loop(0, twice, in_two, 0)
    lax.fori_loop(twice, once, in_one(WIDE), 0)
    lax.fori_loop(once, total // SET, in_one(CHUNK), 0)
    for n in range(count):
        out_parts[n][...] = out_ref[n * ROWS : (n + 1) * ROWS]


def short_attention(shifts, table, after, q_parts, kv_parts):
    count = len(shifts)
    first = table is None
    outs = [jax.ShapeDtypeStruct((ROWS, QW), jnp.bfloat16)] * count
    scratch = [
        pltpu.VMEM((GROUPS * PIECE, KVW), jnp.bfloat16),
        pltpu.VMEM((count * ROWS, QW), jnp.bfloat16),
        pltpu.VMEM((count * ROWS, QW), jnp.bfloat16),
        pltpu.VMEM((SET, GROUP * BLOCK, 2 * HD), jnp.float32),
        pltpu.VMEM((SET, GROUP * BLOCK, HD), jnp.float32),
        pltpu.SMEM((4, count * SB), jnp.int32),
        pltpu.SemaphoreType.DMA((SIDE,)),
        pltpu.SemaphoreType.DMA((count,)),
    ]
    if first:
        outs = outs + [jax.ShapeDtypeStruct((4 * GROUPS, HD), jnp.int32)]
        scratch += [pltpu.VMEM((4 * GROUPS, HD), jnp.int32), pltpu.SemaphoreType.DMA(())]
    found = pl.pallas_call(
        functools.partial(short_kernel, shifts, first, len(after)),
        out_shape=outs,
        in_specs=[HB] * (count + SIDE)
        + [SM if first else HB] * len(after)
        + ([] if first else [SM]),
        out_specs=[VM] * count + ([SM] if first else []),
        scratch_shapes=scratch,
        compiler_params=pltpu.CompilerParams(vmem_limit_bytes=24 * MIB),
        cost_estimate=busy(4 * count),
    )(*q_parts, *kv_parts, *after, *([] if first else [table]))
    return (found[:count], found[count]) if first else (found, table)


def long_kernel(q_in, *refs):
    parts = refs[:5]
    out_ref, token, q_ref, bias_ref, sem = refs[5:]
    copy = pltpu.make_async_copy(q_in, q_ref, sem)
    copy.start()
    token[0] = 0
    square = (LROWS, LROWS)
    lane = lax.broadcasted_iota(jnp.int32, square, 1)
    row = lax.broadcasted_iota(jnp.int32, square, 0)
    docs = [p[LROWS : LROWS + EXTRA, :LROWS].astype(jnp.float32)[:1] for p in parts]
    own_doc = jnp.transpose(jnp.broadcast_to(docs[0], square))
    for n in range(5):
        allowed = own_doc == docs[n]
        if n == 0:
            allowed = allowed & (lane <= row)
        bias_ref[:, n * LROWS : (n + 1) * LROWS] = jnp.where(allowed, 0.0, MASKED)
    copy.wait()

    def one_head(h, _):
        col = pl.multiple_of(h * HD, HD)
        vcol = pl.multiple_of((KVH + h) * HD, HD)
        keys = jnp.concatenate([p[:LROWS, pl.ds(col, HD)] for p in parts], axis=0)
        values = jnp.concatenate([p[:LROWS, pl.ds(vcol, HD)] for p in parts], axis=0)
        for i in range(GROUP):
            qcol = pl.multiple_of((h * GROUP + i) * HD, HD)
            scores = inner(q_ref[:, pl.ds(qcol, HD)], keys) + bias_ref[...]
            out_ref[:, pl.ds(qcol, HD)] = soften(scores, values).astype(jnp.bfloat16)
        return 0

    lax.fori_loop(0, KVH, one_head, 0)


def long_attention(queries, parts):
    return pl.pallas_call(
        long_kernel,
        out_shape=[
            jax.ShapeDtypeStruct((LROWS, QH * HD), jnp.bfloat16),
            jax.ShapeDtypeStruct((1,), jnp.int32),
        ],
        in_specs=[FAR] + [VM] * 5,
        out_specs=[VM, SM],
        scratch_shapes=[
            pltpu.VMEM((LROWS, QH * HD), jnp.bfloat16),
            pltpu.VMEM((LROWS, 5 * LROWS), jnp.float32),
            pltpu.SemaphoreType.DMA(()),
        ],
        compiler_params=pltpu.CompilerParams(vmem_limit_bytes=20 * MIB),
        cost_estimate=busy(0.1),
    )(queries, *parts)


def shards(
    short_queries,
    short_keys,
    short_values,
    block_fill,
    block_home,
    long_queries,
    long_keys,
    long_values,
    long_docs,
):
    *own, own_q, packed = split(
        block_home.reshape(SB),
        block_fill.reshape(SB),
        long_docs.reshape(1, LROWS),
        short_keys.reshape(ROWS, KVH * HD),
        short_values.reshape(ROWS, KVH * HD),
        short_queries.reshape(ROWS, QH * HD),
        long_keys.reshape(LROWS, KVH * HD),
        long_values.reshape(LROWS, KVH * HD),
    )
    sent = {k: send(own[k], along_head(k)) for k in ORDER}
    line_parts = [sent[k] for k in (1, 2, 3)]
    long_one = send(packed, up_chips(1))
    long_two = send(packed, up_chips(2))
    stacked = stack([own[0]] + line_parts)
    sent = {k: send(stacked, along_rows(k)) for k in ORDER[::-1]}
    kv_parts = [stacked] + [sent[k] for k in (1, 2, 3)]
    long_side = send(long_one, other_core)
    core = lax.axis_index("ctx") % 2
    long_cross = send(jnp.where(core == 0, packed, long_two), other_core)
    long_out, token = long_attention(
        long_queries.reshape(LROWS, QH * HD),
        [packed, long_one, long_two, long_side, long_cross],
    )

    mixed, table = short_attention((1, 2, 3), None, [token], line_parts, kv_parts)
    back = [send(piece, along_head(-k)) for k, piece in zip((1, 2, 3), mixed)]
    kept, _ = short_attention((0,), table, [], [own_q], kv_parts)
    short_out = join([kept[0]] + back)
    return short_out.reshape(short_queries.shape), long_out.reshape(long_queries.shape)


def solution(mesh):
    return jax.shard_map(
        shards,
        mesh=mesh,
        in_specs=(
            P("dp", "ctx", None, None),
            P("dp", "ctx", None, None),
            P("dp", "ctx", None, None),
            P("dp", "ctx", None),
            P("dp", "ctx", None),
            P("dp", "ctx", None),
            P("dp", "ctx", None),
            P("dp", "ctx", None),
            P("dp", "ctx"),
        ),
        out_specs=(P("dp", "ctx", None, None), P("dp", "ctx", None)),
        check_vma=False,
    )
```

```python
import functools

import jax
import jax.numpy as jnp
from jax import lax
from jax.experimental import pallas as pl
from jax.experimental.pallas import tpu as pltpu
from jax.sharding import PartitionSpec as P

QH = 16
KVH = 4
HD = 128
BLOCK = 64
SB = 8
GROUP = QH // KVH
SIDE = 4
GROUPS = SIDE * SIDE
RANKS = 8
ROWS = SB * BLOCK
LROWS = 256
EXTRA = 16
PIECE = ROWS + EXTRA
KVW = 2 * HD
QW = GROUP * HD
CHUNK = 4
SET = 4
ORDER = (2, 1, 3)
WIDE = 2 * CHUNK
MASKED = -1e30
SCALE = HD**-0.5 * 1.4426950408889634
MIB = 1024 * 1024

VM = pl.BlockSpec(memory_space=pltpu.VMEM)
SM = pl.BlockSpec(memory_space=pltpu.SMEM)
HB = pl.BlockSpec(memory_space=pl.ANY)
FAR = pl.BlockSpec(memory_space=pltpu.HBM)


def pairs(step):
    found = []
    for x in range(SIDE):
        for y in range(SIDE):
            for z in range(RANKS // 2):
                for core in range(2):
                    target = step(x, y, z, core)
                    if target is not None:
                        tx, ty, tz, tcore = target
                        found.append(
                            (
                                (x * SIDE + y) * RANKS + z * 2 + core,
                                (tx * SIDE + ty) * RANKS + tz * 2 + tcore,
                            )
                        )
    return found


def send(value, step):
    return lax.ppermute(value, ("dp", "ctx"), pairs(step))


def along_head(k):
    def step(x, y, z, core):
        if core == 0:
            return (x + k) % SIDE, y, z, core
        return x, (y + k) % SIDE, z, core

    return step


def along_rows(k):
    def step(x, y, z, core):
        if core == 0:
            return x, (y + k) % SIDE, z, core
        return (x + k) % SIDE, y, z, core

    return step


def up_chips(k):
    def step(x, y, z, core):
        return (x, y, z + k, core) if z + k < RANKS // 2 else None

    return step


def other_core(x, y, z, core):
    return x, y, z, 1 - core


def where_am_i():
    place, rank = lax.axis_index("dp"), lax.axis_index("ctx")
    x, y, core = lax.shift_right_logical(place, 2), place & 3, rank & 1
    return jnp.where(core == 0, x, y), jnp.where(core == 0, y, x), core


def busy(us):
    return pl.CostEstimate(flops=int(us * 1e9), bytes_accessed=MIB, transcendentals=0)


def split_kernel(home_in, fill_in, doc_in, k_ref, v_ref, q_ref, lk_ref, lv_ref, *refs):
    outs, own_q_out, far_q_out, packed_out = refs[:SIDE], *refs[SIDE : SIDE + 3]
    refs = refs[SIDE + 3 :]
    home, fill, docs, pieces, own_q, packed, sems, few_sems, out_sems = refs
    mine = where_am_i()[0]
    few = [
        pltpu.make_async_copy(source, to, few_sems.at[n])
        for n, (source, to) in enumerate(((home_in, home), (fill_in, fill), (doc_in, docs)))
    ]
    for copy in few:
        copy.start()
    copies = {}
    for k in ORDER + (0,):
        head = (mine + k) & 3
        col = pl.multiple_of(head * HD, HD)
        qcol = pl.multiple_of(head * QW, QW)
        piece = pieces.at[k]
        goals = [
            (k_ref.at[:, pl.ds(col, HD)], piece.at[pl.ds(0, ROWS), pl.ds(0, HD)]),
            (v_ref.at[:, pl.ds(col, HD)], piece.at[pl.ds(0, ROWS), pl.ds(HD, HD)]),
            (
                q_ref.at[:, pl.ds(qcol, QW)],
                piece.at[pl.ds(0, ROWS), pl.ds(KVW, QW)] if k else own_q,
            ),
        ]
        copies[k] = [
            pltpu.make_async_copy(source, to, sems.at[k, n]) for n, (source, to) in enumerate(goals)
        ]
        for copy in copies[k]:
            copy.start()
    wide = KVH * HD
    long_copies = [
        pltpu.make_async_copy(
            source, packed.at[pl.ds(0, LROWS), pl.ds(n * wide, wide)], sems.at[SIDE, n]
        )
        for n, source in enumerate((lk_ref, lv_ref))
    ]
    for copy in long_copies:
        copy.start()
    for copy in few:
        copy.wait()
    row = lax.broadcasted_iota(jnp.int32, (EXTRA, KVW), 0)
    facts = jnp.zeros((EXTRA, KVW), jnp.int32)
    for b in range(SB):
        facts = jnp.where(row == b, home[b], facts)
        facts = jnp.where(row == SB + b, fill[b], facts)
    facts = facts.astype(jnp.float32).astype(jnp.bfloat16)
    for k in range(SIDE):
        pieces[k, ROWS:, :KVW] = facts
        if k:
            pieces[k, ROWS:, KVW:] = jnp.zeros((EXTRA, QW), jnp.bfloat16)
    doc_row = docs[...].astype(jnp.float32) + 1.0
    packed[LROWS:, :LROWS] = jnp.broadcast_to(doc_row, (EXTRA, LROWS)).astype(jnp.bfloat16)
    packed[LROWS:, LROWS:] = jnp.zeros((EXTRA, 2 * wide - LROWS), jnp.bfloat16)
    done = []
    for k in ORDER + (0,):
        for copy in copies[k]:
            copy.wait()
        source = pieces.at[k] if k & 1 else pieces.at[k, :, pl.ds(0, KVW)]
        done.append(pltpu.make_async_copy(source, outs[k], out_sems.at[k]))
        done[-1].start()
    far_q = pieces.at[2, pl.ds(0, ROWS), pl.ds(KVW, QW)]
    for n, (source, to) in enumerate(((own_q, own_q_out), (far_q, far_q_out))):
        done.append(pltpu.make_async_copy(source, to, out_sems.at[SIDE + n]))
        done[-1].start()
    for copy in long_copies:
        copy.wait()
    done.append(pltpu.make_async_copy(packed, packed_out, out_sems.at[SIDE + 2]))
    done[-1].start()
    for copy in done:
        copy.wait()


def split(home, fill, docs, keys, values, queries, long_keys, long_values):
    shapes = [(PIECE, KVW + QW if k & 1 else KVW) for k in range(SIDE)]
    shapes += [(ROWS, QW)] * 2 + [(LROWS + EXTRA, 2 * KVH * HD)]
    return pl.pallas_call(
        split_kernel,
        out_shape=[jax.ShapeDtypeStruct(shape, jnp.bfloat16) for shape in shapes],
        in_specs=[FAR] * 8,
        out_specs=[FAR] * (SIDE + 3),
        scratch_shapes=[
            pltpu.SMEM((SB,), jnp.int32),
            pltpu.SMEM((SB,), jnp.int32),
            pltpu.VMEM((1, LROWS), jnp.int32),
            pltpu.VMEM((SIDE, PIECE, KVW + QW), jnp.bfloat16),
            pltpu.VMEM((ROWS, QW), jnp.bfloat16),
            pltpu.VMEM((LROWS + EXTRA, 2 * KVH * HD), jnp.bfloat16),
            pltpu.SemaphoreType.DMA((SIDE + 1, 3)),
            pltpu.SemaphoreType.DMA((3,)),
            pltpu.SemaphoreType.DMA((SIDE + 3,)),
        ],
        compiler_params=pltpu.CompilerParams(vmem_limit_bytes=60 * MIB),
        cost_estimate=busy(2),
    )(home, fill, docs, keys, values, queries, long_keys, long_values)


def join_kernel(*refs):
    pieces, out_ref, sems = refs[:SIDE], refs[SIDE], refs[SIDE + 1]
    mine = where_am_i()[0]
    copies = []
    for k in range(SIDE):
        col = pl.multiple_of(((mine + k) & 3) * QW, QW)
        copies.append(
            pltpu.make_async_copy(pieces[k], out_ref.at[:, pl.ds(col, QW)], sems.at[k])
        )
    for copy in copies:
        copy.start()
    for copy in copies:
        copy.wait()


def join(pieces):
    return pl.pallas_call(
        join_kernel,
        out_shape=jax.ShapeDtypeStruct((ROWS, QH * HD), jnp.bfloat16),
        in_specs=[VM] * SIDE,
        out_specs=FAR,
        scratch_shapes=[pltpu.SemaphoreType.DMA((SIDE,))],
        compiler_params=pltpu.CompilerParams(vmem_limit_bytes=MIB),
        cost_estimate=busy(2),
    )(*pieces)


def fill_table(kv_ref, table_ref):
    head, line, core = where_am_i()
    shape = (GROUPS, HD)
    lane = lax.broadcasted_iota(jnp.int32, shape, 1)
    row = lax.broadcasted_iota(jnp.int32, shape, 0)
    facts = jnp.full(shape, -1.0, jnp.float32)
    for p in range(GROUPS):
        piece = kv_ref[p * PIECE + ROWS : (p + 1) * PIECE, :HD].astype(jnp.float32)
        facts = jnp.where(lane == p, piece, facts)
    facts = facts.astype(jnp.int32)

    def order(p):
        own_head = (head - p) & 3
        own_line = (line - lax.shift_right_logical(p, 2)) & 3
        return jnp.where(core == 0, own_head * SIDE + own_line, own_line * SIDE + own_head)

    one = lax.broadcasted_iota(jnp.int32, (HD, HD), 0)
    two = lax.broadcasted_iota(jnp.int32, (HD, HD), 1)
    earlier = jnp.where((order(one) < order(two)) & (one < GROUPS), 1.0, 0.0)
    here = jnp.zeros(shape, jnp.float32)
    slots = jnp.zeros(shape, jnp.int32)
    fills = jnp.zeros(shape, jnp.int32)
    for b in range(SB):
        same = facts[b : b + 1] == row
        here = jnp.where(same, 1.0, here)
        slots = jnp.where(same, lane * (PIECE // EXTRA) + b * (BLOCK // EXTRA), slots)
        fills = jnp.where(same, facts[SB + b : SB + b + 1], fills)
    ranks = jnp.dot(here, earlier, preferred_element_type=jnp.float32).astype(jnp.int32)
    own_ranks = jnp.zeros((SB, HD), jnp.int32)
    for d in range(GROUPS):
        own_ranks = jnp.where(facts[:SB] == d, ranks[d : d + 1], own_ranks)
    table_ref[: 2 * SB] = facts
    table_ref[2 * SB : 3 * SB] = own_ranks
    table_ref[3 * SB : 4 * SB] = own_ranks
    ranks = jnp.where(here > 0.0, ranks, -1)
    slot_list = jnp.zeros(shape, jnp.int32)
    fill_list = jnp.zeros(shape, jnp.int32)
    for r in range(GROUPS):
        chosen = ranks == r
        slot = jnp.sum(jnp.where(chosen, slots, 0), axis=1, keepdims=True)
        fill = jnp.sum(jnp.where(chosen, fills, 0), axis=1, keepdims=True)
        slot_list = jnp.where(lane == r, slot, slot_list)
        fill_list = jnp.where(lane == r, fill, fill_list)
    table_ref[4 * SB : 4 * SB + GROUPS] = slot_list
    table_ref[4 * SB + GROUPS :] = fill_list


def soften(scores, value_rows):
    row_max = jnp.max(scores, axis=-1, keepdims=True)
    weights = jnp.exp2((scores - row_max) * SCALE)
    totals = jnp.sum(weights, axis=-1, keepdims=True)
    mixture = jnp.dot(
        weights.astype(jnp.bfloat16), value_rows, preferred_element_type=jnp.float32
    )
    return mixture / totals


def inner(queries, key_rows):
    return lax.dot_general(
        queries, key_rows, (((1,), (1,)), ((), ())), preferred_element_type=jnp.float32
    )


def short_kernel(shifts, first, waits, *refs):
    count = len(shifts)
    q_parts, kv_parts = refs[:count], refs[count : count + SIDE]
    refs = refs[count + SIDE + waits :]
    if first:
        out_parts, table = refs[:count], refs[count]
        table_ref, table_sem = refs[-2:]
        refs = refs[count + 1 :]
    else:
        table, out_parts = refs[0], refs[1 : 1 + count]
        refs = refs[1 + count :]
    kv_ref, q_ref, out_ref, mix_ref, top_ref, list_ref, kv_sems, q_sems = refs[:8]
    part_rows = SIDE * PIECE
    copies = [
        pltpu.make_async_copy(
            kv_parts[n], kv_ref.at[pl.ds(n * part_rows, part_rows)], kv_sems.at[n]
        )
        for n in range(SIDE)
    ]
    copies += [
        pltpu.make_async_copy(
            q_parts[n].at[pl.ds(0, ROWS), pl.ds(KVW if k & 1 else 0, QW)],
            q_ref.at[pl.ds(n * ROWS, ROWS)],
            q_sems.at[n],
        )
        for n, k in enumerate(shifts)
    ]
    for copy in copies:
        copy.start()
    for copy in copies:
        copy.wait()
    if first:
        fill_table(kv_ref, table_ref)
        table_copy = pltpu.make_async_copy(table_ref, table, table_sem)
        table_copy.start()
        table_copy.wait()
    low = lax.broadcasted_iota(jnp.int32, (BLOCK, HD), 1) < BLOCK
    lane_row = lax.broadcasted_iota(jnp.int32, (BLOCK, HD), 1) % BLOCK
    row = lax.broadcasted_iota(jnp.int32, (BLOCK, HD), 0)

    total = count * SB
    over = [0, 0, 0]
    ranks = []
    for n in range(total):
        rank = table[2 * SB + n % SB, shifts[0] + n // SB]
        ranks.append(rank)
        over = [old + jnp.where(rank >= 4 * (i + 1), 1, 0) for i, old in enumerate(over)]
    spots = [over[0], over[1], over[2], 0]
    for n in range(total):
        b, k = n % SB, shifts[0] + n // SB
        level = lax.shift_right_logical(ranks[n], 2)
        spot = jnp.where(
            level < 2,
            jnp.where(level == 0, spots[0], spots[1]),
            jnp.where(level == 2, spots[2], spots[3]),
        )
        list_ref[0, spot] = n
        list_ref[1, spot] = table[b, k]
        list_ref[2, spot] = ranks[n]
        list_ref[3, spot] = table[SB + b, k]
        spots = [old + jnp.where(level == i, 1, 0) for i, old in enumerate(spots)]

    def rows_of(at):
        return pl.ds(pl.multiple_of(list_ref[0, at] * BLOCK, BLOCK), BLOCK)

    def scores_of(at, first_key, blocks):
        home, rank = list_ref[1, at], list_ref[2, at]
        q = q_ref[rows_of(at), :]
        q = jnp.concatenate([q[:, h * HD : (h + 1) * HD] for h in range(GROUP)], axis=0)
        fills, shifts_in, keys, values, biases = [], [], [], [], []
        for j in range(blocks):
            n = first_key + j
            start = pl.multiple_of(table[4 * SB + home, n] * EXTRA, EXTRA)
            kv = kv_ref[pl.ds(start, BLOCK), :]
            keys.append(kv[:, :HD])
            values.append(kv[:, HD:])
            fills.append(jnp.where(n <= rank, table[4 * SB + GROUPS + home, n], 0))
            shifts_in.append(jnp.where(n == rank, 1, BLOCK))
        for j in range(0, blocks, 2):
            limit = jnp.minimum(
                jnp.where(low, fills[j], fills[j + 1]),
                row + jnp.where(low, shifts_in[j], shifts_in[j + 1]),
            )
            biases.append(jnp.where(lane_row < limit, 0.0, MASKED))
        scores = inner(q, jnp.concatenate(keys, axis=0))
        scores = scores + jnp.concatenate([jnp.concatenate(biases, axis=1)] * GROUP, axis=0)
        ones = jnp.ones((blocks * BLOCK, HD), jnp.bfloat16)
        return scores, jnp.concatenate([jnp.concatenate(values, axis=0), ones], axis=1)

    def weigh(scores, top, values):
        weights = jnp.exp2((scores - top) * SCALE).astype(jnp.bfloat16)
        return jnp.dot(weights, values, preferred_element_type=jnp.float32)

    def finish(at, mixed):
        mixed = mixed[:, :HD] / mixed[:, HD:]
        used = row < list_ref[3, at]
        for h in range(GROUP):
            part = jnp.where(used, mixed[h * BLOCK : (h + 1) * BLOCK], 0.0)
            out_ref[rows_of(at), h * HD : (h + 1) * HD] = part.astype(jnp.bfloat16)

    def in_one(blocks):
        def body(t, _):
            for u in range(SET):
                at = t * SET + u
                scores, values = scores_of(at, 0, blocks)
                top = jnp.max(scores, axis=-1, keepdims=True)
                finish(at, weigh(scores, top, values))
            return 0

        return body

    def in_two(t, _):
        for u in range(SET):
            scores, values = scores_of(t * SET + u, 0, WIDE)
            top = jnp.max(scores, axis=-1, keepdims=True)
            top_ref[u] = jnp.broadcast_to(top, (GROUP * BLOCK, HD))
            mix_ref[u] = weigh(scores, top, values)
        for u in range(SET):
            scores, values = scores_of(t * SET + u, WIDE, WIDE)
            old = top_ref[u]
            top = jnp.broadcast_to(jnp.max(scores, axis=-1, keepdims=True), old.shape)
            top = jnp.maximum(old, top)
            shrink = jnp.exp2((old - top) * SCALE)
            shrink = jnp.concatenate([shrink, shrink], axis=1)
            top = jnp.concatenate([top] * (WIDE // 2), axis=1)
            finish(t * SET + u, mix_ref[u] * shrink + weigh(scores, top, values))
        return 0

    twice = (over[1] + SET - 1) // SET
    once = (over[0] + SET - 1) // SET
    lax.fori_loop(0, twice, in_two, 0)
    lax.fori_loop(twice, once, in_one(WIDE), 0)
    lax.fori_loop(once, total // SET, in_one(CHUNK), 0)
    for n in range(count):
        out_parts[n][...] = out_ref[n * ROWS : (n + 1) * ROWS]


def short_attention(shifts, table, after, q_parts, kv_parts):
    count = len(shifts)
    first = table is None
    outs = [jax.ShapeDtypeStruct((ROWS, QW), jnp.bfloat16)] * count
    scratch = [
        pltpu.VMEM((GROUPS * PIECE, KVW), jnp.bfloat16),
        pltpu.VMEM((count * ROWS, QW), jnp.bfloat16),
        pltpu.VMEM((count * ROWS, QW), jnp.bfloat16),
        pltpu.VMEM((SET, GROUP * BLOCK, 2 * HD), jnp.float32),
        pltpu.VMEM((SET, GROUP * BLOCK, HD), jnp.float32),
        pltpu.SMEM((4, count * SB), jnp.int32),
        pltpu.SemaphoreType.DMA((SIDE,)),
        pltpu.SemaphoreType.DMA((count,)),
    ]
    if first:
        outs = outs + [jax.ShapeDtypeStruct((4 * GROUPS, HD), jnp.int32)]
        scratch += [pltpu.VMEM((4 * GROUPS, HD), jnp.int32), pltpu.SemaphoreType.DMA(())]
    found = pl.pallas_call(
        functools.partial(short_kernel, shifts, first, len(after)),
        out_shape=outs,
        in_specs=[HB] * (count + SIDE)
        + [SM if first else HB] * len(after)
        + ([] if first else [SM]),
        out_specs=[VM] * count + ([SM] if first else []),
        scratch_shapes=scratch,
        compiler_params=pltpu.CompilerParams(vmem_limit_bytes=24 * MIB),
        cost_estimate=busy(4 * count),
    )(*q_parts, *kv_parts, *after, *([] if first else [table]))
    return (found[:count], found[count]) if first else (found, table)


def long_kernel(q_in, after, *refs):
    parts = refs[:5]
    out_ref, token, q_ref, bias_ref, sem = refs[5:]
    copy = pltpu.make_async_copy(q_in, q_ref, sem)
    copy.start()
    token[0] = 0
    square = (LROWS, LROWS)
    lane = lax.broadcasted_iota(jnp.int32, square, 1)
    row = lax.broadcasted_iota(jnp.int32, square, 0)
    docs = [p[LROWS : LROWS + EXTRA, :LROWS].astype(jnp.float32)[:1] for p in parts]
    own_doc = jnp.transpose(jnp.broadcast_to(docs[0], square))
    for n in range(5):
        allowed = own_doc == docs[n]
        if n == 0:
            allowed = allowed & (lane <= row)
        bias_ref[:, n * LROWS : (n + 1) * LROWS] = jnp.where(allowed, 0.0, MASKED)
    copy.wait()

    def one_head(h, _):
        col = pl.multiple_of(h * HD, HD)
        vcol = pl.multiple_of((KVH + h) * HD, HD)
        keys = jnp.concatenate([p[:LROWS, pl.ds(col, HD)] for p in parts], axis=0)
        values = jnp.concatenate([p[:LROWS, pl.ds(vcol, HD)] for p in parts], axis=0)
        for i in range(GROUP):
            qcol = pl.multiple_of((h * GROUP + i) * HD, HD)
            scores = inner(q_ref[:, pl.ds(qcol, HD)], keys) + bias_ref[...]
            out_ref[:, pl.ds(qcol, HD)] = soften(scores, values).astype(jnp.bfloat16)
        return 0

    lax.fori_loop(0, KVH, one_head, 0)


def long_attention(queries, after, parts):
    return pl.pallas_call(
        long_kernel,
        out_shape=[
            jax.ShapeDtypeStruct((LROWS, QH * HD), jnp.bfloat16),
            jax.ShapeDtypeStruct((1,), jnp.int32),
        ],
        in_specs=[FAR, HB] + [VM] * 5,
        out_specs=[VM, SM],
        scratch_shapes=[
            pltpu.VMEM((LROWS, QH * HD), jnp.bfloat16),
            pltpu.VMEM((LROWS, 5 * LROWS), jnp.float32),
            pltpu.SemaphoreType.DMA(()),
        ],
        compiler_params=pltpu.CompilerParams(vmem_limit_bytes=20 * MIB),
        cost_estimate=busy(0.1),
    )(queries, after, *parts)


def shards(
    short_queries,
    short_keys,
    short_values,
    block_fill,
    block_home,
    long_queries,
    long_keys,
    long_values,
    long_docs,
):
    *own, own_q, far_q, packed = split(
        block_home.reshape(SB),
        block_fill.reshape(SB),
        long_docs.reshape(1, LROWS),
        short_keys.reshape(ROWS, KVH * HD),
        short_values.reshape(ROWS, KVH * HD),
        short_queries.reshape(ROWS, QH * HD),
        long_keys.reshape(LROWS, KVH * HD),
        long_values.reshape(LROWS, KVH * HD),
    )
    sent = {k: send(own[k], along_head(k)) for k in ORDER}
    line_parts = [sent[k] for k in (1, 2, 3)]
    far_q = send(far_q, along_head(2))
    long_one = send(packed, up_chips(1))
    long_two = send(packed, up_chips(2))
    stacked = jnp.concatenate([own[0]] + [part[:, :KVW] for part in line_parts], axis=0)
    sent = {k: send(stacked, along_rows(k)) for k in ORDER[::-1]}
    kv_parts = [stacked] + [sent[k] for k in (1, 2, 3)]
    long_side = send(long_one, other_core)
    core = lax.axis_index("ctx") % 2
    long_cross = send(jnp.where(core == 0, packed, long_two), other_core)
    long_out, token = long_attention(
        long_queries.reshape(LROWS, QH * HD),
        far_q,
        [packed, long_one, long_two, long_side, long_cross],
    )

    mixed, table = short_attention(
        (1, 2, 3), None, [token], [line_parts[0], far_q, line_parts[2]], kv_parts
    )
    back = [send(piece, along_head(-k)) for k, piece in zip((1, 2, 3), mixed)]
    kept, _ = short_attention((0,), table, [], [own_q], kv_parts)
    short_out = join([kept[0]] + back)
    return short_out.reshape(short_queries.shape), long_out.reshape(long_queries.shape)


def solution(mesh):
    return jax.shard_map(
        shards,
        mesh=mesh,
        in_specs=(
            P("dp", "ctx", None, None),
            P("dp", "ctx", None, None),
            P("dp", "ctx", None, None),
            P("dp", "ctx", None),
            P("dp", "ctx", None),
            P("dp", "ctx", None),
            P("dp", "ctx", None),
            P("dp", "ctx", None),
            P("dp", "ctx"),
        ),
        out_specs=(P("dp", "ctx", None, None), P("dp", "ctx", None)),
        check_vma=False,
    )
```

```python
import functools

import jax
import jax.numpy as jnp
from jax import lax
from jax.experimental import pallas as pl
from jax.experimental.pallas import tpu as pltpu
from jax.sharding import PartitionSpec as P

QH = 16
KVH = 4
HD = 128
BLOCK = 64
SB = 8
GROUP = QH // KVH
SIDE = 4
GROUPS = SIDE * SIDE
RANKS = 8
ROWS = SB * BLOCK
LROWS = 256
EXTRA = 16
PIECE = ROWS + EXTRA
KVW = 2 * HD
QW = GROUP * HD
CHUNK = 4
SET = 4
ORDER = (2, 1, 3)
WIDE = 2 * CHUNK
MASKED = -1e30
SCALE = HD**-0.5 * 1.4426950408889634
MIB = 1024 * 1024

VM = pl.BlockSpec(memory_space=pltpu.VMEM)
SM = pl.BlockSpec(memory_space=pltpu.SMEM)
HB = pl.BlockSpec(memory_space=pl.ANY)
FAR = pl.BlockSpec(memory_space=pltpu.HBM)


def pairs(step):
    found = []
    for x in range(SIDE):
        for y in range(SIDE):
            for z in range(RANKS // 2):
                for core in range(2):
                    target = step(x, y, z, core)
                    if target is not None:
                        tx, ty, tz, tcore = target
                        found.append(
                            (
                                (x * SIDE + y) * RANKS + z * 2 + core,
                                (tx * SIDE + ty) * RANKS + tz * 2 + tcore,
                            )
                        )
    return found


def send(value, step):
    return lax.ppermute(value, ("dp", "ctx"), pairs(step))


def along_head(k):
    def step(x, y, z, core):
        if core == 0:
            return (x + k) % SIDE, y, z, core
        return x, (y + k) % SIDE, z, core

    return step


def along_rows(k):
    def step(x, y, z, core):
        if core == 0:
            return x, (y + k) % SIDE, z, core
        return (x + k) % SIDE, y, z, core

    return step


def up_chips(k):
    def step(x, y, z, core):
        return (x, y, z + k, core) if z + k < RANKS // 2 else None

    return step


def other_core(x, y, z, core):
    return x, y, z, 1 - core


def where_am_i():
    place, rank = lax.axis_index("dp"), lax.axis_index("ctx")
    x, y, core = lax.shift_right_logical(place, 2), place & 3, rank & 1
    return jnp.where(core == 0, x, y), jnp.where(core == 0, y, x), core


def busy(us):
    return pl.CostEstimate(flops=int(us * 1e9), bytes_accessed=MIB, transcendentals=0)


def split_kernel(home_in, fill_in, doc_in, k_ref, v_ref, q_ref, lk_ref, lv_ref, *refs):
    outs, own_q_out, far_q_out, packed_out = refs[:SIDE], *refs[SIDE : SIDE + 3]
    refs = refs[SIDE + 3 :]
    home, fill, docs, pieces, own_q, packed, sems, few_sems, out_sems = refs
    mine = where_am_i()[0]
    few = [
        pltpu.make_async_copy(source, to, few_sems.at[n])
        for n, (source, to) in enumerate(((home_in, home), (fill_in, fill), (doc_in, docs)))
    ]
    for copy in few:
        copy.start()
    copies = {}
    for k in ORDER + (0,):
        head = (mine + k) & 3
        col = pl.multiple_of(head * HD, HD)
        qcol = pl.multiple_of(head * QW, QW)
        piece = pieces.at[k]
        goals = [
            (k_ref.at[:, pl.ds(col, HD)], piece.at[pl.ds(0, ROWS), pl.ds(0, HD)]),
            (v_ref.at[:, pl.ds(col, HD)], piece.at[pl.ds(0, ROWS), pl.ds(HD, HD)]),
            (
                q_ref.at[:, pl.ds(qcol, QW)],
                piece.at[pl.ds(0, ROWS), pl.ds(KVW, QW)] if k else own_q,
            ),
        ]
        copies[k] = [
            pltpu.make_async_copy(source, to, sems.at[k, n]) for n, (source, to) in enumerate(goals)
        ]
        for copy in copies[k]:
            copy.start()
    wide = KVH * HD
    long_copies = [
        pltpu.make_async_copy(
            source, packed.at[pl.ds(0, LROWS), pl.ds(n * wide, wide)], sems.at[SIDE, n]
        )
        for n, source in enumerate((lk_ref, lv_ref))
    ]
    for copy in long_copies:
        copy.start()
    for copy in few:
        copy.wait()
    row = lax.broadcasted_iota(jnp.int32, (EXTRA, KVW), 0)
    facts = jnp.zeros((EXTRA, KVW), jnp.int32)
    for b in range(SB):
        facts = jnp.where(row == b, home[b], facts)
        facts = jnp.where(row == SB + b, fill[b], facts)
    facts = facts.astype(jnp.float32).astype(jnp.bfloat16)
    for k in range(SIDE):
        pieces[k, ROWS:, :KVW] = facts
        if k:
            pieces[k, ROWS:, KVW:] = jnp.zeros((EXTRA, QW), jnp.bfloat16)
    doc_row = docs[...].astype(jnp.float32) + 1.0
    packed[LROWS:, :LROWS] = jnp.broadcast_to(doc_row, (EXTRA, LROWS)).astype(jnp.bfloat16)
    packed[LROWS:, LROWS:] = jnp.zeros((EXTRA, 2 * wide - LROWS), jnp.bfloat16)
    done = []
    for k in ORDER + (0,):
        for copy in copies[k]:
            copy.wait()
        source = pieces.at[k] if k & 1 else pieces.at[k, :, pl.ds(0, KVW)]
        done.append(pltpu.make_async_copy(source, outs[k], out_sems.at[k]))
        done[-1].start()
    far_q = pieces.at[2, pl.ds(0, ROWS), pl.ds(KVW, QW)]
    for n, (source, to) in enumerate(((own_q, own_q_out), (far_q, far_q_out))):
        done.append(pltpu.make_async_copy(source, to, out_sems.at[SIDE + n]))
        done[-1].start()
    for copy in long_copies:
        copy.wait()
    done.append(pltpu.make_async_copy(packed, packed_out, out_sems.at[SIDE + 2]))
    done[-1].start()
    for copy in done:
        copy.wait()


def split(home, fill, docs, keys, values, queries, long_keys, long_values):
    shapes = [(PIECE, KVW + QW if k & 1 else KVW) for k in range(SIDE)]
    shapes += [(ROWS, QW)] * 2 + [(LROWS + EXTRA, 2 * KVH * HD)]
    return pl.pallas_call(
        split_kernel,
        out_shape=[jax.ShapeDtypeStruct(shape, jnp.bfloat16) for shape in shapes],
        in_specs=[FAR] * 8,
        out_specs=[FAR] * (SIDE + 3),
        scratch_shapes=[
            pltpu.SMEM((SB,), jnp.int32),
            pltpu.SMEM((SB,), jnp.int32),
            pltpu.VMEM((1, LROWS), jnp.int32),
            pltpu.VMEM((SIDE, PIECE, KVW + QW), jnp.bfloat16),
            pltpu.VMEM((ROWS, QW), jnp.bfloat16),
            pltpu.VMEM((LROWS + EXTRA, 2 * KVH * HD), jnp.bfloat16),
            pltpu.SemaphoreType.DMA((SIDE + 1, 3)),
            pltpu.SemaphoreType.DMA((3,)),
            pltpu.SemaphoreType.DMA((SIDE + 3,)),
        ],
        compiler_params=pltpu.CompilerParams(vmem_limit_bytes=60 * MIB),
        cost_estimate=busy(2),
    )(home, fill, docs, keys, values, queries, long_keys, long_values)


def join_kernel(*refs):
    pieces, out_ref, sems = refs[:SIDE], refs[SIDE], refs[SIDE + 1]
    mine = where_am_i()[0]
    copies = []
    for k in range(SIDE):
        col = pl.multiple_of(((mine + k) & 3) * QW, QW)
        copies.append(
            pltpu.make_async_copy(pieces[k], out_ref.at[:, pl.ds(col, QW)], sems.at[k])
        )
    for copy in copies:
        copy.start()
    for copy in copies:
        copy.wait()


def join(pieces):
    return pl.pallas_call(
        join_kernel,
        out_shape=jax.ShapeDtypeStruct((ROWS, QH * HD), jnp.bfloat16),
        in_specs=[VM] * SIDE,
        out_specs=FAR,
        scratch_shapes=[pltpu.SemaphoreType.DMA((SIDE,))],
        compiler_params=pltpu.CompilerParams(vmem_limit_bytes=MIB),
        cost_estimate=busy(2),
    )(*pieces)


def fill_table(facts_ref, table_ref):
    head, line, core = where_am_i()
    shape = (GROUPS, HD)
    lane = lax.broadcasted_iota(jnp.int32, shape, 1)
    row = lax.broadcasted_iota(jnp.int32, shape, 0)
    facts = jnp.full(shape, -1.0, jnp.float32)
    for p in range(GROUPS):
        piece = facts_ref[p].astype(jnp.float32)
        facts = jnp.where(lane == p, piece, facts)
    facts = facts.astype(jnp.int32)

    def order(p):
        own_head = (head - p) & 3
        own_line = (line - lax.shift_right_logical(p, 2)) & 3
        return jnp.where(core == 0, own_head * SIDE + own_line, own_line * SIDE + own_head)

    one = lax.broadcasted_iota(jnp.int32, (HD, HD), 0)
    two = lax.broadcasted_iota(jnp.int32, (HD, HD), 1)
    earlier = jnp.where((order(one) < order(two)) & (one < GROUPS), 1.0, 0.0)
    here = jnp.zeros(shape, jnp.float32)
    slots = jnp.zeros(shape, jnp.int32)
    fills = jnp.zeros(shape, jnp.int32)
    for b in range(SB):
        same = facts[b : b + 1] == row
        here = jnp.where(same, 1.0, here)
        slots = jnp.where(same, lane * (PIECE // EXTRA) + b * (BLOCK // EXTRA), slots)
        fills = jnp.where(same, facts[SB + b : SB + b + 1], fills)
    ranks = jnp.dot(here, earlier, preferred_element_type=jnp.float32).astype(jnp.int32)
    own_ranks = jnp.zeros((SB, HD), jnp.int32)
    for d in range(GROUPS):
        own_ranks = jnp.where(facts[:SB] == d, ranks[d : d + 1], own_ranks)
    table_ref[: 2 * SB] = facts
    table_ref[2 * SB : 3 * SB] = own_ranks
    table_ref[3 * SB : 4 * SB] = own_ranks
    ranks = jnp.where(here > 0.0, ranks, -1)
    slot_list = jnp.zeros(shape, jnp.int32)
    fill_list = jnp.zeros(shape, jnp.int32)
    for r in range(GROUPS):
        chosen = ranks == r
        slot = jnp.sum(jnp.where(chosen, slots, 0), axis=1, keepdims=True)
        fill = jnp.sum(jnp.where(chosen, fills, 0), axis=1, keepdims=True)
        slot_list = jnp.where(lane == r, slot, slot_list)
        fill_list = jnp.where(lane == r, fill, fill_list)
    table_ref[4 * SB : 4 * SB + GROUPS] = slot_list
    table_ref[4 * SB + GROUPS :] = fill_list


def soften(scores, value_rows):
    row_max = jnp.max(scores, axis=-1, keepdims=True)
    weights = jnp.exp2((scores - row_max) * SCALE)
    totals = jnp.sum(weights, axis=-1, keepdims=True)
    mixture = jnp.dot(
        weights.astype(jnp.bfloat16), value_rows, preferred_element_type=jnp.float32
    )
    return mixture / totals


def inner(queries, key_rows):
    return lax.dot_general(
        queries, key_rows, (((1,), (1,)), ((), ())), preferred_element_type=jnp.float32
    )


def short_kernel(shifts, first, waits, *refs):
    count = len(shifts)
    q_parts, kv_parts = refs[:count], refs[count : count + SIDE]
    refs = refs[count + SIDE + waits :]
    if first:
        out_parts, table = refs[:count], refs[count]
        table_ref, facts_ref, table_sem, facts_sems = refs[-4:]
        refs = refs[count + 1 :]
    else:
        table, out_parts = refs[0], refs[1 : 1 + count]
        refs = refs[1 + count :]
    kv_ref, q_ref, out_ref, mix_ref, top_ref, list_ref, kv_sems, q_sems = refs[:8]
    part_rows = SIDE * PIECE
    copies = [
        pltpu.make_async_copy(
            kv_parts[n], kv_ref.at[pl.ds(n * part_rows, part_rows)], kv_sems.at[n]
        )
        for n in range(SIDE)
    ]
    copies += [
        pltpu.make_async_copy(
            q_parts[n].at[pl.ds(0, ROWS), pl.ds(KVW if k & 1 else 0, QW)],
            q_ref.at[pl.ds(n * ROWS, ROWS)],
            q_sems.at[n],
        )
        for n, k in enumerate(shifts)
    ]
    if first:
        fact_copies = [
            pltpu.make_async_copy(
                kv_parts[p // SIDE].at[
                    pl.ds(p % SIDE * PIECE + ROWS, EXTRA), pl.ds(0, HD)
                ],
                facts_ref.at[p],
                facts_sems.at[p],
            )
            for p in range(GROUPS)
        ]
        for copy in fact_copies:
            copy.start()
    for copy in copies:
        copy.start()
    if first:
        for copy in fact_copies:
            copy.wait()
        fill_table(facts_ref, table_ref)
        table_copy = pltpu.make_async_copy(table_ref, table, table_sem)
        table_copy.start()
        table_copy.wait()
    low = lax.broadcasted_iota(jnp.int32, (BLOCK, HD), 1) < BLOCK
    lane_row = lax.broadcasted_iota(jnp.int32, (BLOCK, HD), 1) % BLOCK
    row = lax.broadcasted_iota(jnp.int32, (BLOCK, HD), 0)

    total = count * SB
    over = [0, 0, 0]
    ranks = []
    for n in range(total):
        rank = table[2 * SB + n % SB, shifts[0] + n // SB]
        ranks.append(rank)
        over = [old + jnp.where(rank >= 4 * (i + 1), 1, 0) for i, old in enumerate(over)]
    spots = [over[0], over[1], over[2], 0]
    for n in range(total):
        b, k = n % SB, shifts[0] + n // SB
        level = lax.shift_right_logical(ranks[n], 2)
        spot = jnp.where(
            level < 2,
            jnp.where(level == 0, spots[0], spots[1]),
            jnp.where(level == 2, spots[2], spots[3]),
        )
        list_ref[0, spot] = n
        list_ref[1, spot] = table[b, k]
        list_ref[2, spot] = ranks[n]
        list_ref[3, spot] = table[SB + b, k]
        spots = [old + jnp.where(level == i, 1, 0) for i, old in enumerate(spots)]

    for copy in copies:
        copy.wait()

    def rows_of(at):
        return pl.ds(pl.multiple_of(list_ref[0, at] * BLOCK, BLOCK), BLOCK)

    def scores_of(at, first_key, blocks):
        home, rank = list_ref[1, at], list_ref[2, at]
        q = q_ref[rows_of(at), :]
        q = jnp.concatenate([q[:, h * HD : (h + 1) * HD] for h in range(GROUP)], axis=0)
        fills, shifts_in, keys, values, biases = [], [], [], [], []
        for j in range(blocks):
            n = first_key + j
            start = pl.multiple_of(table[4 * SB + home, n] * EXTRA, EXTRA)
            kv = kv_ref[pl.ds(start, BLOCK), :]
            keys.append(kv[:, :HD])
            values.append(kv[:, HD:])
            fills.append(jnp.where(n <= rank, table[4 * SB + GROUPS + home, n], 0))
            shifts_in.append(jnp.where(n == rank, 1, BLOCK))
        for j in range(0, blocks, 2):
            limit = jnp.minimum(
                jnp.where(low, fills[j], fills[j + 1]),
                row + jnp.where(low, shifts_in[j], shifts_in[j + 1]),
            )
            biases.append(jnp.where(lane_row < limit, 0.0, MASKED))
        scores = inner(q, jnp.concatenate(keys, axis=0))
        scores = scores + jnp.concatenate([jnp.concatenate(biases, axis=1)] * GROUP, axis=0)
        ones = jnp.ones((blocks * BLOCK, HD), jnp.bfloat16)
        return scores, jnp.concatenate([jnp.concatenate(values, axis=0), ones], axis=1)

    def weigh(scores, top, values):
        weights = jnp.exp2((scores - top) * SCALE).astype(jnp.bfloat16)
        return jnp.dot(weights, values, preferred_element_type=jnp.float32)

    def finish(at, mixed):
        mixed = mixed[:, :HD] / mixed[:, HD:]
        used = row < list_ref[3, at]
        for h in range(GROUP):
            part = jnp.where(used, mixed[h * BLOCK : (h + 1) * BLOCK], 0.0)
            out_ref[rows_of(at), h * HD : (h + 1) * HD] = part.astype(jnp.bfloat16)

    def in_one(blocks):
        def body(t, _):
            for u in range(SET):
                at = t * SET + u
                scores, values = scores_of(at, 0, blocks)
                top = jnp.max(scores, axis=-1, keepdims=True)
                finish(at, weigh(scores, top, values))
            return 0

        return body

    def in_two(t, _):
        for u in range(SET):
            scores, values = scores_of(t * SET + u, 0, WIDE)
            top = jnp.max(scores, axis=-1, keepdims=True)
            top_ref[u] = jnp.broadcast_to(top, (GROUP * BLOCK, HD))
            mix_ref[u] = weigh(scores, top, values)
        for u in range(SET):
            scores, values = scores_of(t * SET + u, WIDE, WIDE)
            old = top_ref[u]
            top = jnp.broadcast_to(jnp.max(scores, axis=-1, keepdims=True), old.shape)
            top = jnp.maximum(old, top)
            shrink = jnp.exp2((old - top) * SCALE)
            shrink = jnp.concatenate([shrink, shrink], axis=1)
            top = jnp.concatenate([top] * (WIDE // 2), axis=1)
            finish(t * SET + u, mix_ref[u] * shrink + weigh(scores, top, values))
        return 0

    twice = (over[1] + SET - 1) // SET
    once = (over[0] + SET - 1) // SET
    lax.fori_loop(0, twice, in_two, 0)
    lax.fori_loop(twice, once, in_one(WIDE), 0)
    lax.fori_loop(once, total // SET, in_one(CHUNK), 0)
    for n in range(count):
        out_parts[n][...] = out_ref[n * ROWS : (n + 1) * ROWS]


def short_attention(shifts, table, after, q_parts, kv_parts):
    count = len(shifts)
    first = table is None
    outs = [jax.ShapeDtypeStruct((ROWS, QW), jnp.bfloat16)] * count
    scratch = [
        pltpu.VMEM((GROUPS * PIECE, KVW), jnp.bfloat16),
        pltpu.VMEM((count * ROWS, QW), jnp.bfloat16),
        pltpu.VMEM((count * ROWS, QW), jnp.bfloat16),
        pltpu.VMEM((SET, GROUP * BLOCK, 2 * HD), jnp.float32),
        pltpu.VMEM((SET, GROUP * BLOCK, HD), jnp.float32),
        pltpu.SMEM((4, count * SB), jnp.int32),
        pltpu.SemaphoreType.DMA((SIDE,)),
        pltpu.SemaphoreType.DMA((count,)),
    ]
    if first:
        outs = outs + [jax.ShapeDtypeStruct((4 * GROUPS, HD), jnp.int32)]
        scratch += [
            pltpu.VMEM((4 * GROUPS, HD), jnp.int32),
            pltpu.VMEM((GROUPS, EXTRA, HD), jnp.bfloat16),
            pltpu.SemaphoreType.DMA(()),
            pltpu.SemaphoreType.DMA((GROUPS,)),
        ]
    found = pl.pallas_call(
        functools.partial(short_kernel, shifts, first, len(after)),
        out_shape=outs,
        in_specs=[HB] * (count + SIDE)
        + [SM if first else HB] * len(after)
        + ([] if first else [SM]),
        out_specs=[VM] * count + ([SM] if first else []),
        scratch_shapes=scratch,
        compiler_params=pltpu.CompilerParams(vmem_limit_bytes=24 * MIB),
        cost_estimate=busy(4 * count),
    )(*q_parts, *kv_parts, *after, *([] if first else [table]))
    return (found[:count], found[count]) if first else (found, table)


def long_kernel(q_in, after, *refs):
    parts = refs[:5]
    out_ref, token, q_ref, bias_ref, sem = refs[5:]
    copy = pltpu.make_async_copy(q_in, q_ref, sem)
    copy.start()
    token[0] = 0
    square = (LROWS, LROWS)
    lane = lax.broadcasted_iota(jnp.int32, square, 1)
    row = lax.broadcasted_iota(jnp.int32, square, 0)
    docs = [p[LROWS : LROWS + EXTRA, :LROWS].astype(jnp.float32)[:1] for p in parts]
    own_doc = jnp.transpose(jnp.broadcast_to(docs[0], square))
    for n in range(5):
        allowed = own_doc == docs[n]
        if n == 0:
            allowed = allowed & (lane <= row)
        bias_ref[:, n * LROWS : (n + 1) * LROWS] = jnp.where(allowed, 0.0, MASKED)
    copy.wait()

    def one_head(h, _):
        col = pl.multiple_of(h * HD, HD)
        vcol = pl.multiple_of((KVH + h) * HD, HD)
        keys = jnp.concatenate([p[:LROWS, pl.ds(col, HD)] for p in parts], axis=0)
        values = jnp.concatenate([p[:LROWS, pl.ds(vcol, HD)] for p in parts], axis=0)
        for i in range(GROUP):
            qcol = pl.multiple_of((h * GROUP + i) * HD, HD)
            scores = inner(q_ref[:, pl.ds(qcol, HD)], keys) + bias_ref[...]
            out_ref[:, pl.ds(qcol, HD)] = soften(scores, values).astype(jnp.bfloat16)
        return 0

    lax.fori_loop(0, KVH, one_head, 0)


def long_attention(queries, after, parts):
    return pl.pallas_call(
        long_kernel,
        out_shape=[
            jax.ShapeDtypeStruct((LROWS, QH * HD), jnp.bfloat16),
            jax.ShapeDtypeStruct((1,), jnp.int32),
        ],
        in_specs=[FAR, HB] + [VM] * 5,
        out_specs=[VM, SM],
        scratch_shapes=[
            pltpu.VMEM((LROWS, QH * HD), jnp.bfloat16),
            pltpu.VMEM((LROWS, 5 * LROWS), jnp.float32),
            pltpu.SemaphoreType.DMA(()),
        ],
        compiler_params=pltpu.CompilerParams(vmem_limit_bytes=20 * MIB),
        cost_estimate=busy(0.1),
    )(queries, after, *parts)


def shards(
    short_queries,
    short_keys,
    short_values,
    block_fill,
    block_home,
    long_queries,
    long_keys,
    long_values,
    long_docs,
):
    *own, own_q, far_q, packed = split(
        block_home.reshape(SB),
        block_fill.reshape(SB),
        long_docs.reshape(1, LROWS),
        short_keys.reshape(ROWS, KVH * HD),
        short_values.reshape(ROWS, KVH * HD),
        short_queries.reshape(ROWS, QH * HD),
        long_keys.reshape(LROWS, KVH * HD),
        long_values.reshape(LROWS, KVH * HD),
    )
    sent = {k: send(own[k], along_head(k)) for k in ORDER}
    line_parts = [sent[k] for k in (1, 2, 3)]
    far_q = send(far_q, along_head(2))
    long_one = send(packed, up_chips(1))
    long_two = send(packed, up_chips(2))
    stacked = jnp.concatenate([own[0]] + [part[:, :KVW] for part in line_parts], axis=0)
    sent = {k: send(stacked, along_rows(k)) for k in ORDER[::-1]}
    kv_parts = [stacked] + [sent[k] for k in (1, 2, 3)]
    long_side = send(long_one, other_core)
    core = lax.axis_index("ctx") % 2
    long_cross = send(jnp.where(core == 0, packed, long_two), other_core)
    long_out, token = long_attention(
        long_queries.reshape(LROWS, QH * HD),
        far_q,
        [packed, long_one, long_two, long_side, long_cross],
    )

    mixed, table = short_attention(
        (1, 2, 3), None, [token], [line_parts[0], far_q, line_parts[2]], kv_parts
    )
    back = [send(piece, along_head(-k)) for k, piece in zip((1, 2, 3), mixed)]
    kept, _ = short_attention((0,), table, [], [own_q], kv_parts)
    short_out = join([kept[0]] + back)
    return short_out.reshape(short_queries.shape), long_out.reshape(long_queries.shape)


def solution(mesh):
    return jax.shard_map(
        shards,
        mesh=mesh,
        in_specs=(
            P("dp", "ctx", None, None),
            P("dp", "ctx", None, None),
            P("dp", "ctx", None, None),
            P("dp", "ctx", None),
            P("dp", "ctx", None),
            P("dp", "ctx", None),
            P("dp", "ctx", None),
            P("dp", "ctx", None),
            P("dp", "ctx"),
        ),
        out_specs=(P("dp", "ctx", None, None), P("dp", "ctx", None)),
        check_vma=False,
    )
```

```python
import functools

import jax
import jax.numpy as jnp
from jax import lax
from jax.experimental import pallas as pl
from jax.experimental.pallas import tpu as pltpu
from jax.sharding import PartitionSpec as P

QH = 16
KVH = 4
HD = 128
BLOCK = 64
SB = 8
GROUP = QH // KVH
SIDE = 4
GROUPS = SIDE * SIDE
RANKS = 8
ROWS = SB * BLOCK
LROWS = 256
EXTRA = 16
PIECE = ROWS + EXTRA
KVW = 2 * HD
QW = GROUP * HD
CHUNK = 4
SET = 4
ORDER = (2, 1, 3)
WIDE = 2 * CHUNK
MASKED = -1e30
SCALE = HD**-0.5 * 1.4426950408889634
MIB = 1024 * 1024

VM = pl.BlockSpec(memory_space=pltpu.VMEM)
SM = pl.BlockSpec(memory_space=pltpu.SMEM)
HB = pl.BlockSpec(memory_space=pl.ANY)
FAR = pl.BlockSpec(memory_space=pltpu.HBM)


def pairs(step):
    found = []
    for x in range(SIDE):
        for y in range(SIDE):
            for z in range(RANKS // 2):
                for core in range(2):
                    target = step(x, y, z, core)
                    if target is not None:
                        tx, ty, tz, tcore = target
                        found.append(
                            (
                                (x * SIDE + y) * RANKS + z * 2 + core,
                                (tx * SIDE + ty) * RANKS + tz * 2 + tcore,
                            )
                        )
    return found


def send(value, step):
    return lax.ppermute(value, ("dp", "ctx"), pairs(step))


def along_head(k):
    def step(x, y, z, core):
        if core == 0:
            return (x + k) % SIDE, y, z, core
        return x, (y + k) % SIDE, z, core

    return step


def along_rows(k):
    def step(x, y, z, core):
        if core == 0:
            return x, (y + k) % SIDE, z, core
        return (x + k) % SIDE, y, z, core

    return step


def up_chips(k):
    def step(x, y, z, core):
        return (x, y, z + k, core) if z + k < RANKS // 2 else None

    return step


def other_core(x, y, z, core):
    return x, y, z, 1 - core


def where_am_i():
    place, rank = lax.axis_index("dp"), lax.axis_index("ctx")
    x, y, core = lax.shift_right_logical(place, 2), place & 3, rank & 1
    return jnp.where(core == 0, x, y), jnp.where(core == 0, y, x), core


def busy(us):
    return pl.CostEstimate(flops=int(us * 1e9), bytes_accessed=MIB, transcendentals=0)


def split_kernel(home_in, fill_in, doc_in, k_ref, v_ref, q_ref, lk_ref, lv_ref, *refs):
    outs, own_q_out, far_q_out, packed_out = refs[:SIDE], *refs[SIDE : SIDE + 3]
    refs = refs[SIDE + 3 :]
    home, fill, docs, pieces, own_q, packed, sems, few_sems, out_sems = refs
    mine = where_am_i()[0]
    few = [
        pltpu.make_async_copy(source, to, few_sems.at[n])
        for n, (source, to) in enumerate(((home_in, home), (fill_in, fill), (doc_in, docs)))
    ]
    for copy in few:
        copy.start()
    copies = {}
    for k in ORDER + (0,):
        head = (mine + k) & 3
        col = pl.multiple_of(head * HD, HD)
        qcol = pl.multiple_of(head * QW, QW)
        piece = pieces.at[k]
        goals = [
            (k_ref.at[:, pl.ds(col, HD)], piece.at[pl.ds(0, ROWS), pl.ds(0, HD)]),
            (v_ref.at[:, pl.ds(col, HD)], piece.at[pl.ds(0, ROWS), pl.ds(HD, HD)]),
            (
                q_ref.at[:, pl.ds(qcol, QW)],
                piece.at[pl.ds(0, ROWS), pl.ds(KVW, QW)] if k else own_q,
            ),
        ]
        copies[k] = [
            pltpu.make_async_copy(source, to, sems.at[k, n]) for n, (source, to) in enumerate(goals)
        ]
        for copy in copies[k]:
            copy.start()
    wide = KVH * HD
    long_copies = [
        pltpu.make_async_copy(
            source, packed.at[pl.ds(0, LROWS), pl.ds(n * wide, wide)], sems.at[SIDE, n]
        )
        for n, source in enumerate((lk_ref, lv_ref))
    ]
    for copy in long_copies:
        copy.start()
    for copy in few:
        copy.wait()
    row = lax.broadcasted_iota(jnp.int32, (EXTRA, KVW), 0)
    facts = jnp.zeros((EXTRA, KVW), jnp.int32)
    for b in range(SB):
        facts = jnp.where(row == b, home[b], facts)
        facts = jnp.where(row == SB + b, fill[b], facts)
    facts = facts.astype(jnp.float32).astype(jnp.bfloat16)
    for k in range(SIDE):
        pieces[k, ROWS:, :KVW] = facts
        if k:
            pieces[k, ROWS:, KVW:] = jnp.zeros((EXTRA, QW), jnp.bfloat16)
    doc_row = docs[...].astype(jnp.float32) + 1.0
    packed[LROWS:, :LROWS] = jnp.broadcast_to(doc_row, (EXTRA, LROWS)).astype(jnp.bfloat16)
    packed[LROWS:, LROWS:] = jnp.zeros((EXTRA, 2 * wide - LROWS), jnp.bfloat16)
    done = []
    for k in ORDER + (0,):
        for copy in copies[k]:
            copy.wait()
        source = pieces.at[k] if k & 1 else pieces.at[k, :, pl.ds(0, KVW)]
        done.append(pltpu.make_async_copy(source, outs[k], out_sems.at[k]))
        done[-1].start()
    far_q = pieces.at[2, pl.ds(0, ROWS), pl.ds(KVW, QW)]
    for n, (source, to) in enumerate(((own_q, own_q_out), (far_q, far_q_out))):
        done.append(pltpu.make_async_copy(source, to, out_sems.at[SIDE + n]))
        done[-1].start()
    for copy in long_copies:
        copy.wait()
    done.append(pltpu.make_async_copy(packed, packed_out, out_sems.at[SIDE + 2]))
    done[-1].start()
    for copy in done:
        copy.wait()


def split(home, fill, docs, keys, values, queries, long_keys, long_values):
    shapes = [(PIECE, KVW + QW if k & 1 else KVW) for k in range(SIDE)]
    shapes += [(ROWS, QW)] * 2 + [(LROWS + EXTRA, 2 * KVH * HD)]
    return pl.pallas_call(
        split_kernel,
        out_shape=[jax.ShapeDtypeStruct(shape, jnp.bfloat16) for shape in shapes],
        in_specs=[FAR] * 8,
        out_specs=[FAR] * (SIDE + 3),
        scratch_shapes=[
            pltpu.SMEM((SB,), jnp.int32),
            pltpu.SMEM((SB,), jnp.int32),
            pltpu.VMEM((1, LROWS), jnp.int32),
            pltpu.VMEM((SIDE, PIECE, KVW + QW), jnp.bfloat16),
            pltpu.VMEM((ROWS, QW), jnp.bfloat16),
            pltpu.VMEM((LROWS + EXTRA, 2 * KVH * HD), jnp.bfloat16),
            pltpu.SemaphoreType.DMA((SIDE + 1, 3)),
            pltpu.SemaphoreType.DMA((3,)),
            pltpu.SemaphoreType.DMA((SIDE + 3,)),
        ],
        compiler_params=pltpu.CompilerParams(vmem_limit_bytes=60 * MIB),
        cost_estimate=busy(2),
    )(home, fill, docs, keys, values, queries, long_keys, long_values)


def join_kernel(*refs):
    pieces, out_ref, sems = refs[:SIDE], refs[SIDE], refs[SIDE + 1]
    mine = where_am_i()[0]
    copies = []
    for k in range(SIDE):
        col = pl.multiple_of(((mine + k) & 3) * QW, QW)
        copies.append(
            pltpu.make_async_copy(pieces[k], out_ref.at[:, pl.ds(col, QW)], sems.at[k])
        )
    for copy in copies:
        copy.start()
    for copy in copies:
        copy.wait()


def join(pieces):
    return pl.pallas_call(
        join_kernel,
        out_shape=jax.ShapeDtypeStruct((ROWS, QH * HD), jnp.bfloat16),
        in_specs=[VM] * SIDE,
        out_specs=FAR,
        scratch_shapes=[pltpu.SemaphoreType.DMA((SIDE,))],
        compiler_params=pltpu.CompilerParams(vmem_limit_bytes=MIB),
        cost_estimate=busy(2),
    )(*pieces)


def fill_table(facts_ref, table_ref):
    head, line, core = where_am_i()
    shape = (GROUPS, HD)
    lane = lax.broadcasted_iota(jnp.int32, shape, 1)
    row = lax.broadcasted_iota(jnp.int32, shape, 0)
    facts = jnp.full(shape, -1.0, jnp.float32)
    for p in range(GROUPS):
        piece = facts_ref[p].astype(jnp.float32)
        facts = jnp.where(lane == p, piece, facts)
    facts = facts.astype(jnp.int32)

    def order(p):
        own_head = (head - p) & 3
        own_line = (line - lax.shift_right_logical(p, 2)) & 3
        return jnp.where(core == 0, own_head * SIDE + own_line, own_line * SIDE + own_head)

    one = lax.broadcasted_iota(jnp.int32, (HD, HD), 0)
    two = lax.broadcasted_iota(jnp.int32, (HD, HD), 1)
    earlier = jnp.where((order(one) < order(two)) & (one < GROUPS), 1.0, 0.0)
    here = jnp.zeros(shape, jnp.float32)
    slots = jnp.zeros(shape, jnp.int32)
    fills = jnp.zeros(shape, jnp.int32)
    for b in range(SB):
        same = facts[b : b + 1] == row
        here = jnp.where(same, 1.0, here)
        slots = jnp.where(same, lane * (PIECE // EXTRA) + b * (BLOCK // EXTRA), slots)
        fills = jnp.where(same, facts[SB + b : SB + b + 1], fills)
    ranks = jnp.dot(here, earlier, preferred_element_type=jnp.float32).astype(jnp.int32)
    own_ranks = jnp.zeros((SB, HD), jnp.int32)
    for d in range(GROUPS):
        own_ranks = jnp.where(facts[:SB] == d, ranks[d : d + 1], own_ranks)
    table_ref[: 2 * SB] = facts
    table_ref[2 * SB : 3 * SB] = own_ranks
    table_ref[3 * SB : 4 * SB] = own_ranks
    ranks = jnp.where(here > 0.0, ranks, -1)
    slot_list = jnp.zeros(shape, jnp.int32)
    fill_list = jnp.zeros(shape, jnp.int32)
    for r in range(GROUPS):
        chosen = ranks == r
        slot = jnp.sum(jnp.where(chosen, slots, 0), axis=1, keepdims=True)
        fill = jnp.sum(jnp.where(chosen, fills, 0), axis=1, keepdims=True)
        slot_list = jnp.where(lane == r, slot, slot_list)
        fill_list = jnp.where(lane == r, fill, fill_list)
    table_ref[4 * SB : 4 * SB + GROUPS] = slot_list
    table_ref[4 * SB + GROUPS :] = fill_list


def inner(queries, key_rows):
    return lax.dot_general(
        queries, key_rows, (((1,), (1,)), ((), ())), preferred_element_type=jnp.float32
    )


def short_kernel(shifts, first, waits, *refs):
    count = len(shifts)
    q_parts, kv_parts = refs[:count], refs[count : count + SIDE]
    refs = refs[count + SIDE + waits :]
    if first:
        out_parts, table = refs[:count], refs[count]
        table_ref, facts_ref, table_sem, facts_sems = refs[-4:]
        refs = refs[count + 1 :]
    else:
        table, out_parts = refs[0], refs[1 : 1 + count]
        refs = refs[1 + count :]
    kv_ref, q_ref, out_ref, mix_ref, top_ref, list_ref, kv_sems, q_sems = refs[:8]
    part_rows = SIDE * PIECE
    copies = [
        pltpu.make_async_copy(
            kv_parts[n], kv_ref.at[pl.ds(n * part_rows, part_rows)], kv_sems.at[n]
        )
        for n in range(SIDE)
    ]
    copies += [
        pltpu.make_async_copy(
            q_parts[n].at[pl.ds(0, ROWS), pl.ds(KVW if k & 1 else 0, QW)],
            q_ref.at[pl.ds(n * ROWS, ROWS)],
            q_sems.at[n],
        )
        for n, k in enumerate(shifts)
    ]
    if first:
        fact_copies = [
            pltpu.make_async_copy(
                kv_parts[p // SIDE].at[
                    pl.ds(p % SIDE * PIECE + ROWS, EXTRA), pl.ds(0, HD)
                ],
                facts_ref.at[p],
                facts_sems.at[p],
            )
            for p in range(GROUPS)
        ]
        for copy in fact_copies:
            copy.start()
    for copy in copies:
        copy.start()
    if first:
        for copy in fact_copies:
            copy.wait()
        fill_table(facts_ref, table_ref)
        table_copy = pltpu.make_async_copy(table_ref, table, table_sem)
        table_copy.start()
        table_copy.wait()
    low = lax.broadcasted_iota(jnp.int32, (BLOCK, HD), 1) < BLOCK
    lane_row = lax.broadcasted_iota(jnp.int32, (BLOCK, HD), 1) % BLOCK
    row = lax.broadcasted_iota(jnp.int32, (BLOCK, HD), 0)

    total = count * SB
    over = [0, 0, 0]
    ranks = []
    for n in range(total):
        rank = table[2 * SB + n % SB, shifts[0] + n // SB]
        ranks.append(rank)
        over = [old + jnp.where(rank >= 4 * (i + 1), 1, 0) for i, old in enumerate(over)]
    spots = [over[0], over[1], over[2], 0]
    for n in range(total):
        b, k = n % SB, shifts[0] + n // SB
        level = lax.shift_right_logical(ranks[n], 2)
        spot = jnp.where(
            level < 2,
            jnp.where(level == 0, spots[0], spots[1]),
            jnp.where(level == 2, spots[2], spots[3]),
        )
        list_ref[0, spot] = n
        list_ref[1, spot] = table[b, k]
        list_ref[2, spot] = ranks[n]
        list_ref[3, spot] = table[SB + b, k]
        spots = [old + jnp.where(level == i, 1, 0) for i, old in enumerate(spots)]

    for copy in copies:
        copy.wait()

    def rows_of(at):
        return pl.ds(pl.multiple_of(list_ref[0, at] * BLOCK, BLOCK), BLOCK)

    def scores_of(at, first_key, blocks):
        home, rank = list_ref[1, at], list_ref[2, at]
        q = q_ref[rows_of(at), :]
        q = jnp.concatenate([q[:, h * HD : (h + 1) * HD] for h in range(GROUP)], axis=0)
        fills, shifts_in, keys, values, biases = [], [], [], [], []
        for j in range(blocks):
            n = first_key + j
            start = pl.multiple_of(table[4 * SB + home, n] * EXTRA, EXTRA)
            kv = kv_ref[pl.ds(start, BLOCK), :]
            keys.append(kv[:, :HD])
            values.append(kv[:, HD:])
            fills.append(jnp.where(n <= rank, table[4 * SB + GROUPS + home, n], 0))
            shifts_in.append(jnp.where(n == rank, 1, BLOCK))
        for j in range(0, blocks, 2):
            limit = jnp.minimum(
                jnp.where(low, fills[j], fills[j + 1]),
                row + jnp.where(low, shifts_in[j], shifts_in[j + 1]),
            )
            biases.append(jnp.where(lane_row < limit, 0.0, MASKED))
        scores = inner(q, jnp.concatenate(keys, axis=0))
        scores = scores + jnp.concatenate([jnp.concatenate(biases, axis=1)] * GROUP, axis=0)
        ones = jnp.ones((blocks * BLOCK, HD), jnp.bfloat16)
        return scores, jnp.concatenate([jnp.concatenate(values, axis=0), ones], axis=1)

    def weigh(scores, top, values):
        weights = jnp.exp2((scores - top) * SCALE).astype(jnp.bfloat16)
        return jnp.dot(weights, values, preferred_element_type=jnp.float32)

    def finish(at, mixed):
        mixed = mixed[:, :HD] / mixed[:, HD:]
        used = row < list_ref[3, at]
        for h in range(GROUP):
            part = jnp.where(used, mixed[h * BLOCK : (h + 1) * BLOCK], 0.0)
            out_ref[rows_of(at), h * HD : (h + 1) * HD] = part.astype(jnp.bfloat16)

    def in_one(blocks):
        def body(t, _):
            for u in range(SET):
                at = t * SET + u
                scores, values = scores_of(at, 0, blocks)
                top = jnp.max(scores, axis=-1, keepdims=True)
                finish(at, weigh(scores, top, values))
            return 0

        return body

    def in_two(t, _):
        for u in range(SET):
            scores, values = scores_of(t * SET + u, 0, WIDE)
            top = jnp.max(scores, axis=-1, keepdims=True)
            top_ref[u] = jnp.broadcast_to(top, (GROUP * BLOCK, HD))
            mix_ref[u] = weigh(scores, top, values)
        for u in range(SET):
            scores, values = scores_of(t * SET + u, WIDE, WIDE)
            old = top_ref[u]
            top = jnp.broadcast_to(jnp.max(scores, axis=-1, keepdims=True), old.shape)
            top = jnp.maximum(old, top)
            shrink = jnp.exp2((old - top) * SCALE)
            shrink = jnp.concatenate([shrink, shrink], axis=1)
            top = jnp.concatenate([top] * (WIDE // 2), axis=1)
            finish(t * SET + u, mix_ref[u] * shrink + weigh(scores, top, values))
        return 0

    twice = (over[1] + SET - 1) // SET
    once = (over[0] + SET - 1) // SET
    lax.fori_loop(0, twice, in_two, 0)
    lax.fori_loop(twice, once, in_one(WIDE), 0)
    lax.fori_loop(once, total // SET, in_one(CHUNK), 0)
    for n in range(count):
        out_parts[n][...] = out_ref[n * ROWS : (n + 1) * ROWS]


def short_attention(shifts, table, after, q_parts, kv_parts):
    count = len(shifts)
    first = table is None
    outs = [jax.ShapeDtypeStruct((ROWS, QW), jnp.bfloat16)] * count
    scratch = [
        pltpu.VMEM((GROUPS * PIECE, KVW), jnp.bfloat16),
        pltpu.VMEM((count * ROWS, QW), jnp.bfloat16),
        pltpu.VMEM((count * ROWS, QW), jnp.bfloat16),
        pltpu.VMEM((SET, GROUP * BLOCK, 2 * HD), jnp.float32),
        pltpu.VMEM((SET, GROUP * BLOCK, HD), jnp.float32),
        pltpu.SMEM((4, count * SB), jnp.int32),
        pltpu.SemaphoreType.DMA((SIDE,)),
        pltpu.SemaphoreType.DMA((count,)),
    ]
    if first:
        outs = outs + [jax.ShapeDtypeStruct((4 * GROUPS, HD), jnp.int32)]
        scratch += [
            pltpu.VMEM((4 * GROUPS, HD), jnp.int32),
            pltpu.VMEM((GROUPS, EXTRA, HD), jnp.bfloat16),
            pltpu.SemaphoreType.DMA(()),
            pltpu.SemaphoreType.DMA((GROUPS,)),
        ]
    found = pl.pallas_call(
        functools.partial(short_kernel, shifts, first, len(after)),
        out_shape=outs,
        in_specs=[HB] * (count + SIDE)
        + [SM if first else HB] * len(after)
        + ([] if first else [SM]),
        out_specs=[VM] * count + ([SM] if first else []),
        scratch_shapes=scratch,
        compiler_params=pltpu.CompilerParams(vmem_limit_bytes=24 * MIB),
        cost_estimate=busy(4 * count),
    )(*q_parts, *kv_parts, *after, *([] if first else [table]))
    return (found[:count], found[count]) if first else (found, table)


def long_kernel(q_in, after, *refs):
    parts = list(refs[:5])
    out_ref, token, q_ref, bias_ref, sem = refs[5:]
    copy = pltpu.make_async_copy(q_in, q_ref, sem)
    copy.start()
    token[0] = 0
    square = (LROWS, LROWS)
    lane = lax.broadcasted_iota(jnp.int32, square, 1)
    row = lax.broadcasted_iota(jnp.int32, square, 0)
    docs = [p[LROWS : LROWS + EXTRA, :LROWS].astype(jnp.float32)[:1] for p in parts]
    own_doc = jnp.transpose(jnp.broadcast_to(docs[0], square))
    for n in range(5):
        allowed = own_doc == docs[n]
        if n == 0:
            allowed = allowed & (lane <= row)
        at = (n + 4) % 5 * LROWS
        bias_ref[:, at : at + LROWS] = jnp.where(allowed, 0.0, MASKED)
    copy.wait()

    def one_head(h, _):
        col = pl.multiple_of(h * HD, HD)
        vcol = pl.multiple_of((KVH + h) * HD, HD)
        order = parts[1:] + parts[:1]
        keys = jnp.concatenate([p[:LROWS, pl.ds(col, HD)] for p in order], axis=0)
        values = jnp.concatenate([p[:LROWS, pl.ds(vcol, HD)] for p in order], axis=0)
        values = jnp.concatenate([values, jnp.ones((5 * LROWS, HD), jnp.bfloat16)], axis=1)
        for i in range(GROUP):
            qcol = pl.multiple_of((h * GROUP + i) * HD, HD)
            for half in range(2):
                rows = slice(half * HD, (half + 1) * HD)
                seen = (8 + half + 1) * HD
                scores = inner(q_ref[rows, pl.ds(qcol, HD)], keys[:seen])
                scores = scores + bias_ref[rows, :seen]
                top = jnp.max(scores, axis=-1, keepdims=True)
                weights = jnp.exp2((scores - top) * SCALE).astype(jnp.bfloat16)
                mixed = jnp.dot(weights, values[:seen], preferred_element_type=jnp.float32)
                mixed = mixed[:, :HD] / mixed[:, HD:]
                out_ref[rows, pl.ds(qcol, HD)] = mixed.astype(jnp.bfloat16)
        return 0

    lax.fori_loop(0, KVH, one_head, 0)


def long_attention(queries, after, parts):
    return pl.pallas_call(
        long_kernel,
        out_shape=[
            jax.ShapeDtypeStruct((LROWS, QH * HD), jnp.bfloat16),
            jax.ShapeDtypeStruct((1,), jnp.int32),
        ],
        in_specs=[FAR, HB] + [VM] * 5,
        out_specs=[VM, SM],
        scratch_shapes=[
            pltpu.VMEM((LROWS, QH * HD), jnp.bfloat16),
            pltpu.VMEM((LROWS, 5 * LROWS), jnp.float32),
            pltpu.SemaphoreType.DMA(()),
        ],
        compiler_params=pltpu.CompilerParams(vmem_limit_bytes=20 * MIB),
        cost_estimate=busy(0.1),
    )(queries, after, *parts)


def shards(
    short_queries,
    short_keys,
    short_values,
    block_fill,
    block_home,
    long_queries,
    long_keys,
    long_values,
    long_docs,
):
    *own, own_q, far_q, packed = split(
        block_home.reshape(SB),
        block_fill.reshape(SB),
        long_docs.reshape(1, LROWS),
        short_keys.reshape(ROWS, KVH * HD),
        short_values.reshape(ROWS, KVH * HD),
        short_queries.reshape(ROWS, QH * HD),
        long_keys.reshape(LROWS, KVH * HD),
        long_values.reshape(LROWS, KVH * HD),
    )
    sent = {k: send(own[k], along_head(k)) for k in ORDER}
    line_parts = [sent[k] for k in (1, 2, 3)]
    far_q = send(far_q, along_head(2))
    long_one = send(packed, up_chips(1))
    long_two = send(packed, up_chips(2))
    stacked = jnp.concatenate([own[0]] + [part[:, :KVW] for part in line_parts], axis=0)
    sent = {k: send(stacked, along_rows(k)) for k in ORDER[::-1]}
    kv_parts = [stacked] + [sent[k] for k in (1, 2, 3)]
    long_side = send(long_one, other_core)
    core = lax.axis_index("ctx") % 2
    long_cross = send(jnp.where(core == 0, packed, long_two), other_core)
    long_out, token = long_attention(
        long_queries.reshape(LROWS, QH * HD),
        far_q,
        [packed, long_one, long_two, long_side, long_cross],
    )

    mixed, table = short_attention(
        (1, 2, 3), None, [token], [line_parts[0], far_q, line_parts[2]], kv_parts
    )
    back = [send(piece, along_head(-k)) for k, piece in zip((1, 2, 3), mixed)]
    kept, _ = short_attention((0,), table, [], [own_q], kv_parts)
    short_out = join([kept[0]] + back)
    return short_out.reshape(short_queries.shape), long_out.reshape(long_queries.shape)


def solution(mesh):
    return jax.shard_map(
        shards,
        mesh=mesh,
        in_specs=(
            P("dp", "ctx", None, None),
            P("dp", "ctx", None, None),
            P("dp", "ctx", None, None),
            P("dp", "ctx", None),
            P("dp", "ctx", None),
            P("dp", "ctx", None),
            P("dp", "ctx", None),
            P("dp", "ctx", None),
            P("dp", "ctx"),
        ),
        out_specs=(P("dp", "ctx", None, None), P("dp", "ctx", None)),
        check_vma=False,
    )
```

```python
import functools

import jax
import jax.numpy as jnp
from jax import lax
from jax.experimental import pallas as pl
from jax.experimental.pallas import tpu as pltpu
from jax.sharding import PartitionSpec as P

QH = 16
KVH = 4
HD = 128
BLOCK = 64
SB = 8
GROUP = QH // KVH
SIDE = 4
GROUPS = SIDE * SIDE
RANKS = 8
ROWS = SB * BLOCK
LROWS = 256
EXTRA = 16
PIECE = ROWS + EXTRA
KVW = 2 * HD
QW = GROUP * HD
CHUNK = 4
SET = 4
ORDER = (2, 1, 3)
WIDE = 2 * CHUNK
MASKED = -1e30
SCALE = HD**-0.5 * 1.4426950408889634
MIB = 1024 * 1024

VM = pl.BlockSpec(memory_space=pltpu.VMEM)
SM = pl.BlockSpec(memory_space=pltpu.SMEM)
HB = pl.BlockSpec(memory_space=pl.ANY)
FAR = pl.BlockSpec(memory_space=pltpu.HBM)


def pairs(step):
    found = []
    for x in range(SIDE):
        for y in range(SIDE):
            for z in range(RANKS // 2):
                for core in range(2):
                    target = step(x, y, z, core)
                    if target is not None:
                        tx, ty, tz, tcore = target
                        found.append(
                            (
                                (x * SIDE + y) * RANKS + z * 2 + core,
                                (tx * SIDE + ty) * RANKS + tz * 2 + tcore,
                            )
                        )
    return found


def send(value, step):
    return lax.ppermute(value, ("dp", "ctx"), pairs(step))


def along_head(k):
    def step(x, y, z, core):
        if core == 0:
            return (x + k) % SIDE, y, z, core
        return x, (y + k) % SIDE, z, core

    return step


def along_rows(k):
    def step(x, y, z, core):
        if core == 0:
            return x, (y + k) % SIDE, z, core
        return (x + k) % SIDE, y, z, core

    return step


def up_chips(k):
    def step(x, y, z, core):
        return (x, y, z + k, core) if z + k < RANKS // 2 else None

    return step


def other_core(x, y, z, core):
    return x, y, z, 1 - core


def where_am_i():
    place, rank = lax.axis_index("dp"), lax.axis_index("ctx")
    x, y, core = lax.shift_right_logical(place, 2), place & 3, rank & 1
    return jnp.where(core == 0, x, y), jnp.where(core == 0, y, x), core


def busy(us):
    return pl.CostEstimate(flops=int(us * 1e9), bytes_accessed=MIB, transcendentals=0)


def split_kernel(home_in, fill_in, doc_in, k_ref, v_ref, q_ref, lk_ref, lv_ref, *refs):
    outs, own_q_out, far_q_out, packed_out = refs[:SIDE], *refs[SIDE : SIDE + 3]
    refs = refs[SIDE + 3 :]
    home, fill, docs, pieces, own_q, packed, sems, few_sems, out_sems = refs
    mine = where_am_i()[0]
    few = [
        pltpu.make_async_copy(source, to, few_sems.at[n])
        for n, (source, to) in enumerate(((home_in, home), (fill_in, fill), (doc_in, docs)))
    ]
    for copy in few:
        copy.start()
    copies = {}
    for k in ORDER + (0,):
        head = (mine + k) & 3
        col = pl.multiple_of(head * HD, HD)
        qcol = pl.multiple_of(head * QW, QW)
        piece = pieces.at[k]
        goals = [
            (k_ref.at[:, pl.ds(col, HD)], piece.at[pl.ds(0, ROWS), pl.ds(0, HD)]),
            (v_ref.at[:, pl.ds(col, HD)], piece.at[pl.ds(0, ROWS), pl.ds(HD, HD)]),
            (
                q_ref.at[:, pl.ds(qcol, QW)],
                piece.at[pl.ds(0, ROWS), pl.ds(KVW, QW)] if k else own_q,
            ),
        ]
        copies[k] = [
            pltpu.make_async_copy(source, to, sems.at[k, n]) for n, (source, to) in enumerate(goals)
        ]
        for copy in copies[k]:
            copy.start()
    wide = KVH * HD
    long_copies = [
        pltpu.make_async_copy(
            source, packed.at[pl.ds(0, LROWS), pl.ds(n * wide, wide)], sems.at[SIDE, n]
        )
        for n, source in enumerate((lk_ref, lv_ref))
    ]
    for copy in long_copies:
        copy.start()
    for copy in few:
        copy.wait()
    row = lax.broadcasted_iota(jnp.int32, (EXTRA, KVW), 0)
    facts = jnp.zeros((EXTRA, KVW), jnp.int32)
    for b in range(SB):
        facts = jnp.where(row == b, home[b], facts)
        facts = jnp.where(row == SB + b, fill[b], facts)
    facts = facts.astype(jnp.float32).astype(jnp.bfloat16)
    for k in range(SIDE):
        pieces[k, ROWS:, :KVW] = facts
        if k:
            pieces[k, ROWS:, KVW:] = jnp.zeros((EXTRA, QW), jnp.bfloat16)
    doc_row = docs[...].astype(jnp.float32) + 1.0
    packed[LROWS:, :LROWS] = jnp.broadcast_to(doc_row, (EXTRA, LROWS)).astype(jnp.bfloat16)
    packed[LROWS:, LROWS:] = jnp.zeros((EXTRA, 2 * wide - LROWS), jnp.bfloat16)
    done = []
    for k in ORDER + (0,):
        for copy in copies[k]:
            copy.wait()
        source = pieces.at[k] if k & 1 else pieces.at[k, :, pl.ds(0, KVW)]
        done.append(pltpu.make_async_copy(source, outs[k], out_sems.at[k]))
        done[-1].start()
    far_q = pieces.at[2, pl.ds(0, ROWS), pl.ds(KVW, QW)]
    for n, (source, to) in enumerate(((own_q, own_q_out), (far_q, far_q_out))):
        done.append(pltpu.make_async_copy(source, to, out_sems.at[SIDE + n]))
        done[-1].start()
    for copy in long_copies:
        copy.wait()
    done.append(pltpu.make_async_copy(packed, packed_out, out_sems.at[SIDE + 2]))
    done[-1].start()
    for copy in done:
        copy.wait()


def split(home, fill, docs, keys, values, queries, long_keys, long_values):
    shapes = [(PIECE, KVW + QW if k & 1 else KVW) for k in range(SIDE)]
    shapes += [(ROWS, QW)] * 2 + [(LROWS + EXTRA, 2 * KVH * HD)]
    return pl.pallas_call(
        split_kernel,
        out_shape=[jax.ShapeDtypeStruct(shape, jnp.bfloat16) for shape in shapes],
        in_specs=[FAR] * 8,
        out_specs=[FAR] * (SIDE + 3),
        scratch_shapes=[
            pltpu.SMEM((SB,), jnp.int32),
            pltpu.SMEM((SB,), jnp.int32),
            pltpu.VMEM((1, LROWS), jnp.int32),
            pltpu.VMEM((SIDE, PIECE, KVW + QW), jnp.bfloat16),
            pltpu.VMEM((ROWS, QW), jnp.bfloat16),
            pltpu.VMEM((LROWS + EXTRA, 2 * KVH * HD), jnp.bfloat16),
            pltpu.SemaphoreType.DMA((SIDE + 1, 3)),
            pltpu.SemaphoreType.DMA((3,)),
            pltpu.SemaphoreType.DMA((SIDE + 3,)),
        ],
        compiler_params=pltpu.CompilerParams(vmem_limit_bytes=60 * MIB),
        cost_estimate=busy(2),
    )(home, fill, docs, keys, values, queries, long_keys, long_values)


def join_kernel(*refs):
    pieces, out_ref, sems = refs[:SIDE], refs[SIDE], refs[SIDE + 1]
    mine = where_am_i()[0]
    copies = []
    for k in range(SIDE):
        col = pl.multiple_of(((mine + k) & 3) * QW, QW)
        copies.append(
            pltpu.make_async_copy(pieces[k], out_ref.at[:, pl.ds(col, QW)], sems.at[k])
        )
    for copy in copies:
        copy.start()
    for copy in copies:
        copy.wait()


def join(pieces):
    return pl.pallas_call(
        join_kernel,
        out_shape=jax.ShapeDtypeStruct((ROWS, QH * HD), jnp.bfloat16),
        in_specs=[VM] * SIDE,
        out_specs=FAR,
        scratch_shapes=[pltpu.SemaphoreType.DMA((SIDE,))],
        compiler_params=pltpu.CompilerParams(vmem_limit_bytes=MIB),
        cost_estimate=busy(2),
    )(*pieces)


def fill_table(facts_ref, table_ref):
    head, line, core = where_am_i()
    shape = (GROUPS, HD)
    lane = lax.broadcasted_iota(jnp.int32, shape, 1)
    row = lax.broadcasted_iota(jnp.int32, shape, 0)
    facts = jnp.full(shape, -1.0, jnp.float32)
    for p in range(GROUPS):
        piece = facts_ref[p].astype(jnp.float32)
        facts = jnp.where(lane == p, piece, facts)
    facts = facts.astype(jnp.int32)

    def order(p):
        own_head = (head - p) & 3
        own_line = (line - lax.shift_right_logical(p, 2)) & 3
        return jnp.where(core == 0, own_head * SIDE + own_line, own_line * SIDE + own_head)

    one = lax.broadcasted_iota(jnp.int32, (HD, HD), 0)
    two = lax.broadcasted_iota(jnp.int32, (HD, HD), 1)
    earlier = jnp.where((order(one) < order(two)) & (one < GROUPS), 1.0, 0.0)
    here = jnp.zeros(shape, jnp.float32)
    slots = jnp.zeros(shape, jnp.int32)
    fills = jnp.zeros(shape, jnp.int32)
    for b in range(SB):
        same = facts[b : b + 1] == row
        here = jnp.where(same, 1.0, here)
        slots = jnp.where(same, lane * (PIECE // EXTRA) + b * (BLOCK // EXTRA), slots)
        fills = jnp.where(same, facts[SB + b : SB + b + 1], fills)
    ranks = jnp.dot(here, earlier, preferred_element_type=jnp.float32).astype(jnp.int32)
    own_ranks = jnp.zeros((SB, HD), jnp.int32)
    for d in range(GROUPS):
        own_ranks = jnp.where(facts[:SB] == d, ranks[d : d + 1], own_ranks)
    table_ref[: 2 * SB] = facts
    table_ref[2 * SB : 3 * SB] = own_ranks
    table_ref[3 * SB : 4 * SB] = own_ranks
    ranks = jnp.where(here > 0.0, ranks, -1)
    slot_list = jnp.zeros(shape, jnp.int32)
    fill_list = jnp.zeros(shape, jnp.int32)
    for r in range(GROUPS):
        chosen = ranks == r
        slot = jnp.sum(jnp.where(chosen, slots, 0), axis=1, keepdims=True)
        fill = jnp.sum(jnp.where(chosen, fills, 0), axis=1, keepdims=True)
        slot_list = jnp.where(lane == r, slot, slot_list)
        fill_list = jnp.where(lane == r, fill, fill_list)
    table_ref[4 * SB : 4 * SB + GROUPS] = slot_list
    table_ref[4 * SB + GROUPS :] = fill_list


def inner(queries, key_rows):
    return lax.dot_general(
        queries, key_rows, (((1,), (1,)), ((), ())), preferred_element_type=jnp.float32
    )


def short_kernel(shifts, first, waits, *refs):
    count = len(shifts)
    q_parts, kv_parts = refs[:count], refs[count : count + SIDE]
    refs = refs[count + SIDE + waits :]
    if first:
        out_parts, table = refs[:count], refs[count]
        table_ref, facts_ref, table_sem, facts_sems = refs[-4:]
        refs = refs[count + 1 :]
    else:
        table, out_parts = refs[0], refs[1 : 1 + count]
        refs = refs[1 + count :]
    kv_ref, q_ref, out_ref, mix_ref, top_ref, list_ref, kv_sems, q_sems = refs[:8]
    part_rows = SIDE * PIECE
    copies = [
        pltpu.make_async_copy(
            kv_parts[n], kv_ref.at[pl.ds(n * part_rows, part_rows)], kv_sems.at[n]
        )
        for n in range(SIDE)
    ]
    copies += [
        pltpu.make_async_copy(
            q_parts[n].at[pl.ds(0, ROWS), pl.ds(KVW if k & 1 else 0, QW)],
            q_ref.at[pl.ds(n * ROWS, ROWS)],
            q_sems.at[n],
        )
        for n, k in enumerate(shifts)
    ]
    if first:
        fact_copies = [
            pltpu.make_async_copy(
                kv_parts[p // SIDE].at[
                    pl.ds(p % SIDE * PIECE + ROWS, EXTRA), pl.ds(0, HD)
                ],
                facts_ref.at[p],
                facts_sems.at[p],
            )
            for p in range(GROUPS)
        ]
        for copy in fact_copies:
            copy.start()
    for copy in copies:
        copy.start()
    if first:
        for copy in fact_copies:
            copy.wait()
        fill_table(facts_ref, table_ref)
        table_copy = pltpu.make_async_copy(table_ref, table, table_sem)
        table_copy.start()
        table_copy.wait()
    low = lax.broadcasted_iota(jnp.int32, (BLOCK, HD), 1) < BLOCK
    lane_row = lax.broadcasted_iota(jnp.int32, (BLOCK, HD), 1) % BLOCK
    row = lax.broadcasted_iota(jnp.int32, (BLOCK, HD), 0)

    total = count * SB
    over = [0, 0, 0]
    ranks = []
    for n in range(total):
        rank = table[2 * SB + n % SB, shifts[n // SB]]
        ranks.append(rank)
        over = [old + jnp.where(rank >= 4 * (i + 1), 1, 0) for i, old in enumerate(over)]
    spots = [over[0], over[1], over[2], 0]
    for n in range(total):
        b, k = n % SB, shifts[n // SB]
        level = lax.shift_right_logical(ranks[n], 2)
        spot = jnp.where(
            level < 2,
            jnp.where(level == 0, spots[0], spots[1]),
            jnp.where(level == 2, spots[2], spots[3]),
        )
        list_ref[0, spot] = n
        list_ref[1, spot] = table[b, k]
        list_ref[2, spot] = ranks[n]
        list_ref[3, spot] = table[SB + b, k]
        spots = [old + jnp.where(level == i, 1, 0) for i, old in enumerate(spots)]

    for copy in copies:
        copy.wait()

    def rows_of(at):
        return pl.ds(pl.multiple_of(list_ref[0, at] * BLOCK, BLOCK), BLOCK)

    def scores_of(at, first_key, blocks):
        home, rank = list_ref[1, at], list_ref[2, at]
        q = q_ref[rows_of(at), :]
        q = jnp.concatenate([q[:, h * HD : (h + 1) * HD] for h in range(GROUP)], axis=0)
        fills, shifts_in, keys, values, biases = [], [], [], [], []
        for j in range(blocks):
            n = first_key + j
            start = pl.multiple_of(table[4 * SB + home, n] * EXTRA, EXTRA)
            kv = kv_ref[pl.ds(start, BLOCK), :]
            keys.append(kv[:, :HD])
            values.append(kv[:, HD:])
            fills.append(jnp.where(n <= rank, table[4 * SB + GROUPS + home, n], 0))
            shifts_in.append(jnp.where(n == rank, 1, BLOCK))
        for j in range(0, blocks, 2):
            limit = jnp.minimum(
                jnp.where(low, fills[j], fills[j + 1]),
                row + jnp.where(low, shifts_in[j], shifts_in[j + 1]),
            )
            biases.append(jnp.where(lane_row < limit, 0.0, MASKED))
        scores = inner(q, jnp.concatenate(keys, axis=0))
        scores = scores + jnp.concatenate([jnp.concatenate(biases, axis=1)] * GROUP, axis=0)
        ones = jnp.ones((blocks * BLOCK, HD), jnp.bfloat16)
        return scores, jnp.concatenate([jnp.concatenate(values, axis=0), ones], axis=1)

    def weigh(scores, top, values):
        weights = jnp.exp2((scores - top) * SCALE).astype(jnp.bfloat16)
        return jnp.dot(weights, values, preferred_element_type=jnp.float32)

    def finish(at, mixed):
        mixed = mixed[:, :HD] / mixed[:, HD:]
        used = row < list_ref[3, at]
        for h in range(GROUP):
            part = jnp.where(used, mixed[h * BLOCK : (h + 1) * BLOCK], 0.0)
            out_ref[rows_of(at), h * HD : (h + 1) * HD] = part.astype(jnp.bfloat16)

    def in_one(blocks):
        def body(t, _):
            for u in range(SET):
                at = t * SET + u
                scores, values = scores_of(at, 0, blocks)
                top = jnp.max(scores, axis=-1, keepdims=True)
                finish(at, weigh(scores, top, values))
            return 0

        return body

    def in_two(t, _):
        for u in range(SET):
            scores, values = scores_of(t * SET + u, 0, WIDE)
            top = jnp.max(scores, axis=-1, keepdims=True)
            top_ref[u] = jnp.broadcast_to(top, (GROUP * BLOCK, HD))
            mix_ref[u] = weigh(scores, top, values)
        for u in range(SET):
            scores, values = scores_of(t * SET + u, WIDE, WIDE)
            old = top_ref[u]
            top = jnp.broadcast_to(jnp.max(scores, axis=-1, keepdims=True), old.shape)
            top = jnp.maximum(old, top)
            shrink = jnp.exp2((old - top) * SCALE)
            shrink = jnp.concatenate([shrink, shrink], axis=1)
            top = jnp.concatenate([top] * (WIDE // 2), axis=1)
            finish(t * SET + u, mix_ref[u] * shrink + weigh(scores, top, values))
        return 0

    twice = (over[1] + SET - 1) // SET
    once = (over[0] + SET - 1) // SET
    lax.fori_loop(0, twice, in_two, 0)
    lax.fori_loop(twice, once, in_one(WIDE), 0)
    lax.fori_loop(once, total // SET, in_one(CHUNK), 0)
    for n in range(count):
        out_parts[n][...] = out_ref[n * ROWS : (n + 1) * ROWS]


def short_attention(shifts, table, after, q_parts, kv_parts):
    count = len(shifts)
    first = table is None
    outs = [jax.ShapeDtypeStruct((ROWS, QW), jnp.bfloat16)] * count
    scratch = [
        pltpu.VMEM((GROUPS * PIECE, KVW), jnp.bfloat16),
        pltpu.VMEM((count * ROWS, QW), jnp.bfloat16),
        pltpu.VMEM((count * ROWS, QW), jnp.bfloat16),
        pltpu.VMEM((SET, GROUP * BLOCK, 2 * HD), jnp.float32),
        pltpu.VMEM((SET, GROUP * BLOCK, HD), jnp.float32),
        pltpu.SMEM((4, count * SB), jnp.int32),
        pltpu.SemaphoreType.DMA((SIDE,)),
        pltpu.SemaphoreType.DMA((count,)),
    ]
    if first:
        outs = outs + [jax.ShapeDtypeStruct((4 * GROUPS, HD), jnp.int32)]
        scratch += [
            pltpu.VMEM((4 * GROUPS, HD), jnp.int32),
            pltpu.VMEM((GROUPS, EXTRA, HD), jnp.bfloat16),
            pltpu.SemaphoreType.DMA(()),
            pltpu.SemaphoreType.DMA((GROUPS,)),
        ]
    found = pl.pallas_call(
        functools.partial(short_kernel, shifts, first, len(after)),
        out_shape=outs,
        in_specs=[HB] * (count + SIDE)
        + [SM if first else HB] * len(after)
        + ([] if first else [SM]),
        out_specs=[VM] * count + ([SM] if first else []),
        scratch_shapes=scratch,
        compiler_params=pltpu.CompilerParams(vmem_limit_bytes=24 * MIB),
        cost_estimate=busy(30),
    )(*q_parts, *kv_parts, *after, *([] if first else [table]))
    return (found[:count], found[count]) if first else (found, table)


def long_kernel(q_in, after, *refs):
    parts = list(refs[:5])
    out_ref, token, q_ref, bias_ref, sem = refs[5:]
    copy = pltpu.make_async_copy(q_in, q_ref, sem)
    copy.start()
    token[0] = 0
    square = (LROWS, LROWS)
    lane = lax.broadcasted_iota(jnp.int32, square, 1)
    row = lax.broadcasted_iota(jnp.int32, square, 0)
    docs = [p[LROWS : LROWS + EXTRA, :LROWS].astype(jnp.float32)[:1] for p in parts]
    own_doc = jnp.transpose(jnp.broadcast_to(docs[0], square))
    for n in range(5):
        allowed = own_doc == docs[n]
        if n == 0:
            allowed = allowed & (lane <= row)
        at = (n + 4) % 5 * LROWS
        bias_ref[:, at : at + LROWS] = jnp.where(allowed, 0.0, MASKED)
    copy.wait()

    def one_head(h, _):
        col = pl.multiple_of(h * HD, HD)
        vcol = pl.multiple_of((KVH + h) * HD, HD)
        order = parts[1:] + parts[:1]
        keys = jnp.concatenate([p[:LROWS, pl.ds(col, HD)] for p in order], axis=0)
        values = jnp.concatenate([p[:LROWS, pl.ds(vcol, HD)] for p in order], axis=0)
        values = jnp.concatenate([values, jnp.ones((5 * LROWS, HD), jnp.bfloat16)], axis=1)
        for i in range(GROUP):
            qcol = pl.multiple_of((h * GROUP + i) * HD, HD)
            for half in range(2):
                rows = slice(half * HD, (half + 1) * HD)
                seen = (8 + half + 1) * HD
                scores = inner(q_ref[rows, pl.ds(qcol, HD)], keys[:seen])
                scores = scores + bias_ref[rows, :seen]
                top = jnp.max(scores, axis=-1, keepdims=True)
                weights = jnp.exp2((scores - top) * SCALE).astype(jnp.bfloat16)
                mixed = jnp.dot(weights, values[:seen], preferred_element_type=jnp.float32)
                mixed = mixed[:, :HD] / mixed[:, HD:]
                out_ref[rows, pl.ds(qcol, HD)] = mixed.astype(jnp.bfloat16)
        return 0

    lax.fori_loop(0, KVH, one_head, 0)


def long_attention(queries, after, parts):
    return pl.pallas_call(
        long_kernel,
        out_shape=[
            jax.ShapeDtypeStruct((LROWS, QH * HD), jnp.bfloat16),
            jax.ShapeDtypeStruct((1,), jnp.int32),
        ],
        in_specs=[FAR, HB] + [VM] * 5,
        out_specs=[VM, SM],
        scratch_shapes=[
            pltpu.VMEM((LROWS, QH * HD), jnp.bfloat16),
            pltpu.VMEM((LROWS, 5 * LROWS), jnp.float32),
            pltpu.SemaphoreType.DMA(()),
        ],
        compiler_params=pltpu.CompilerParams(vmem_limit_bytes=20 * MIB),
        cost_estimate=busy(0.1),
    )(queries, after, *parts)


def shards(
    short_queries,
    short_keys,
    short_values,
    block_fill,
    block_home,
    long_queries,
    long_keys,
    long_values,
    long_docs,
):
    *own, own_q, far_q, packed = split(
        block_home.reshape(SB),
        block_fill.reshape(SB),
        long_docs.reshape(1, LROWS),
        short_keys.reshape(ROWS, KVH * HD),
        short_values.reshape(ROWS, KVH * HD),
        short_queries.reshape(ROWS, QH * HD),
        long_keys.reshape(LROWS, KVH * HD),
        long_values.reshape(LROWS, KVH * HD),
    )
    sent = {k: send(own[k], along_head(k)) for k in ORDER}
    line_parts = [sent[k] for k in (1, 2, 3)]
    far_q = send(far_q, along_head(2))
    long_one = send(packed, up_chips(1))
    long_two = send(packed, up_chips(2))
    stacked = jnp.concatenate([own[0]] + [part[:, :KVW] for part in line_parts], axis=0)
    sent = {k: send(stacked, along_rows(k)) for k in ORDER[::-1]}
    kv_parts = [stacked] + [sent[k] for k in (1, 2, 3)]
    long_side = send(long_one, other_core)
    core = lax.axis_index("ctx") % 2
    long_cross = send(jnp.where(core == 0, packed, long_two), other_core)
    long_out, token = long_attention(
        long_queries.reshape(LROWS, QH * HD),
        far_q,
        [packed, long_one, long_two, long_side, long_cross],
    )

    q_parts = {1: line_parts[0], 2: far_q, 3: line_parts[2]}
    back, table = {}, None
    for shifts in ((1, 2), (3,)):
        mixed, table = short_attention(
            shifts, table, [] if table is not None else [token], [q_parts[k] for k in shifts], kv_parts
        )
        for k, piece in zip(shifts, mixed):
            back[k] = send(piece, along_head(-k))
    back = [back[k] for k in (1, 2, 3)]
    kept, _ = short_attention((0,), table, [], [own_q], kv_parts)
    short_out = join([kept[0]] + back)
    return short_out.reshape(short_queries.shape), long_out.reshape(long_queries.shape)


def solution(mesh):
    return jax.shard_map(
        shards,
        mesh=mesh,
        in_specs=(
            P("dp", "ctx", None, None),
            P("dp", "ctx", None, None),
            P("dp", "ctx", None, None),
            P("dp", "ctx", None),
            P("dp", "ctx", None),
            P("dp", "ctx", None),
            P("dp", "ctx", None),
            P("dp", "ctx", None),
            P("dp", "ctx"),
        ),
        out_specs=(P("dp", "ctx", None, None), P("dp", "ctx", None)),
        check_vma=False,
    )
```
